256 devices in a mesh: chan: 32 (over z, y_lo, core), bin: 8 (over y_hi, x).
Axes of the slice: x: 4, y: 4 (y_hi: 2, y_lo: 2; y = y_hi * 2 + y_lo), z: 8, core: 2. Of those that a mesh axis runs over, the one named last changes fastest.
Arguments:
- traces: float32 [6144, 4096], P(('chan', 'bin')), may hold values from -6 to 6
- fir_taps: float32 [64], replicated, may hold values from -0.75 to 0.75
- pair_bin: int32 [6144, 6144], P(('chan', 'bin')), may hold values from 0 to 63, as said below
Outputs:
- stacks: float32 [64, 512], P('bin')
The draws below stay inside these ranges and needn't reach their ends.
Inputs may be any that keep to these rules, and one draw needn't show every extreme that they name: pair_bin[a, b] equals pair_bin[b, a].
All inputs are finite; a program needn't handle non-finite values.
Results may differ from the reference program's by a relative error of at most 0.0051.
Values may be sent and summed in bfloat16 or wider, within the bound.
A program may use at most 320 MiB of HBM per device.

```python
import math
import jax
import jax.numpy as jnp
import numpy as np
from jax import lax

SAMPLES = 4096
TAPS = 64
BAND_LO = 64
NF = 192
MARGIN = 32
LAGS = 512
NBINS = 64
CHANNELS = 6144


def draw_pair_bin(key, part):
    key = jax.random.fold_in(key, 11)
    raw = jax.random.randint(key, (CHANNELS, CHANNELS), 0, NBINS, dtype=jnp.int32)
    row_index = jnp.arange(CHANNELS, dtype=jnp.int32)[:, None]
    col_index = jnp.arange(CHANNELS, dtype=jnp.int32)[None, :]
    return jnp.where(row_index < col_index, raw, raw.T)


def block_scale(stream_key, dims, split, least, largest):
    gain = 1.0
    for dim, blocks in split:
        heights = jax.random.uniform(jax.random.fold_in(jax.random.fold_in(stream_key, 6), dim), (blocks,), jnp.float32, least / len(split), largest / len(split))
        gain = gain * jnp.repeat(jnp.exp(heights), dims[dim] // blocks).reshape((-1,) + (1,) * (len(dims) - 1 - dim))
    return gain


def noise(stream_key, shape, spread, most, split=(), kind=jnp.bfloat16):
    values = spread * jax.random.normal(stream_key, shape, jnp.float32)
    if split:
        values = values * block_scale(stream_key, shape, split, -0.22, 0.18)
    return jnp.clip(values, -most, most).astype(kind)


def setup_inputs(seed: int = 0) -> dict:
    streams_of = jax.random.split(jax.random.key(seed), 4)
    traces = noise(streams_of[0], (CHANNELS, SAMPLES), 1.0, 6.0, ((0, 256),), jnp.float32)
    fir_taps = noise(streams_of[1], (TAPS,), TAPS ** -0.5, 0.75, (), jnp.float32)
    pair_bin = draw_pair_bin(jax.random.fold_in(streams_of[3], 71), 0)
    return dict(traces=traces, fir_taps=fir_taps, pair_bin=pair_bin)


def whiten(traces, fir_taps):
    filtered = jnp.zeros_like(traces)
    for shift_count in range(TAPS):
        moved = jnp.pad(traces[:, :SAMPLES - shift_count], ((0, 0), (shift_count, 0)))
        filtered = filtered + fir_taps[shift_count] * moved
    spectrum = jnp.fft.rfft(filtered, axis=-1)
    extended = spectrum[:, BAND_LO - MARGIN:BAND_LO + NF + MARGIN]
    ext_re = jnp.real(extended).astype(jnp.float32)
    ext_im = jnp.imag(extended).astype(jnp.float32)
    power = ext_re * ext_re + ext_im * ext_im
    smooth = jnp.zeros((traces.shape[0], NF), jnp.float32)
    for offset in range(2 * MARGIN):
        smooth = smooth + power[:, offset:offset + NF]
    smooth = smooth / (2.0 * MARGIN)
    scale = 1.0 / jnp.sqrt(smooth + 1e-06)
    band_re = ext_re[:, MARGIN:MARGIN + NF] * scale
    band_im = ext_im[:, MARGIN:MARGIN + NF] * scale
    return jnp.concatenate([band_re, band_im], axis=1).astype(jnp.bfloat16)

def lag_table():
    freq = BAND_LO + jnp.arange(NF, dtype=jnp.int32)
    lag = jnp.arange(LAGS, dtype=jnp.int32) - LAGS // 2
    phase = freq[:, None] * lag[None, :] % SAMPLES
    angle = 2.0 * math.pi / SAMPLES * phase.astype(jnp.float32)
    return jnp.concatenate([jnp.cos(angle), -jnp.sin(angle)], axis=0) * (2.0 / SAMPLES)

def reference(traces, fir_taps, pair_bin):
    white = whiten(traces, fir_taps)
    block = math.gcd(CHANNELS, 128)
    count = CHANNELS // block
    first_list = []
    second_list = []
    for first in range(count):
        for second in range(first, count):
            first_list.append(first)
            second_list.append(second)
    firsts = jnp.asarray(np.array(first_list, dtype=np.int32))
    seconds = jnp.asarray(np.array(second_list, dtype=np.int32))
    codes = jnp.arange(NBINS, dtype=jnp.int32)

    def visit(index, total):
        start_a = firsts[index] * block
        start_b = seconds[index] * block
        left = lax.dynamic_slice_in_dim(white, start_a, block, 0).astype(jnp.float32)
        right = lax.dynamic_slice_in_dim(white, start_b, block, 0).astype(jnp.float32)
        ar, ai = (left[:, :NF], left[:, NF:])
        br, bi = (right[:, :NF], right[:, NF:])
        real_part = ar[:, None, :] * br[None, :, :] + ai[:, None, :] * bi[None, :, :]
        imag_part = ai[:, None, :] * br[None, :, :] - ar[:, None, :] * bi[None, :, :]
        cross = jnp.concatenate([real_part, imag_part], axis=2).astype(jnp.bfloat16).reshape(block * block, 2 * NF)
        rows_bins = lax.dynamic_slice(pair_bin, (start_a, start_b), (block, block))
        index_a = start_a + jnp.arange(block, dtype=jnp.int32)
        index_b = start_b + jnp.arange(block, dtype=jnp.int32)
        keep = index_a[:, None] < index_b[None, :]
        onehot = ((rows_bins[:, :, None] == codes[None, None, :]) & keep[:, :, None]).astype(jnp.bfloat16).reshape(block * block, NBINS)
        return total + lax.dot_general(onehot, cross, (((0,), (0,)), ((), ())), preferred_element_type=jnp.float32)
    total = lax.fori_loop(0, len(first_list), visit, jnp.zeros((NBINS, 2 * NF), jnp.float32))
    return jnp.dot(total, lag_table(), precision=lax.Precision.HIGHEST)
```

```python
import math

import jax
import jax.numpy as jnp
import ml_dtypes
import numpy as np
from jax import lax
from jax.experimental import pallas as pl
from jax.experimental.pallas import tpu as pltpu
from jax.sharding import PartitionSpec as P

SAMPLES = 4096
TAPS = 64
BAND_LO = 64
NF = 192
MARGIN = 32
LAGS = 512
NBINS = 64
ROWS = 24
LEVEL = 768
MESH = pl.DeviceIdType.MESH
F32 = jnp.float32
BF16 = jnp.bfloat16


def lane_freqs():
    lane = np.arange(128)
    return np.concatenate([16 * (lane % 16) + 8 * j + lane // 16 for j in range(2)])


def split2(table):
    hi = table.astype(ml_dtypes.bfloat16)
    lo = (table - hi.astype(np.float64)).astype(ml_dtypes.bfloat16)
    return hi, lo


def make_tables():
    e = lane_freqs()
    u = np.arange(256)
    ang = 2 * math.pi / SAMPLES * ((u[None, :] * np.arange(16)[:, None]) % SAMPLES)
    twiddle = np.concatenate([np.cos(ang), np.sin(ang)], 0).astype(np.float32)
    p = 2 + np.arange(128) % 16
    ang = 2 * math.pi / 256 * ((u[:, None] * p[None, :]) % 256)
    c, s = np.cos(ang), np.sin(ang)
    fine = np.concatenate([np.concatenate([c, -s], 1), np.concatenate([s, c], 1)], 0)
    ang = 2 * math.pi / SAMPLES * ((np.arange(128)[:, None] * (32 + e)[None, :]) % SAMPLES)
    taps = np.concatenate([np.cos(ang), -np.sin(ang)], 1)
    taps[TAPS:] = 0.0
    window = ((e[:, None] >= e[None, :] - MARGIN) & (e[:, None] < e[None, :] + MARGIN)) / (2.0 * MARGIN)
    f = e - MARGIN
    ok = (f >= 0) & (f < NF)
    phase = ((BAND_LO + np.where(ok, f, 0))[:, None] * (np.arange(LAGS) - LAGS // 2)[None, :]) % SAMPLES
    ang = 2 * math.pi / SAMPLES * phase
    lag = np.concatenate([np.cos(ang), -np.sin(ang)], 0) * (2.0 / SAMPLES) * np.concatenate([ok, ok])[:, None]
    return (twiddle, *split2(fine), taps.astype(np.float32), window.astype(ml_dtypes.bfloat16), *split2(lag))


def dot(a, b, **kw):
    return jnp.dot(a, b, preferred_element_type=F32, **kw)


def halves(a):
    hi = a.astype(BF16)
    return hi, (a - hi.astype(F32)).astype(BF16)


def sixteen(x):
    root = math.sqrt(0.5)
    a = [x[k] + x[k + 8] for k in range(8)]
    b = [x[k] - x[k + 8] for k in range(8)]
    c = [a[k] + a[k + 4] for k in range(4)]
    d = [a[k] - a[k + 4] for k in range(4)]
    y = [None] * 9
    zero = jnp.zeros_like(x[0])
    even, odd = c[0] + c[2], c[1] + c[3]
    y[0] = (even + odd, zero)
    y[8] = (even - odd, zero)
    y[4] = (c[0] - c[2], c[3] - c[1])
    m, n = (d[1] - d[3]) * root, (d[1] + d[3]) * root
    y[2] = (d[0] + m, -(n + d[2]))
    y[6] = (d[0] - m, d[2] - n)
    for r in (1, 3, 5, 7):
        re, im = b[0], b[4] * (-1.0 if r % 4 == 1 else 1.0)
        for k in (1, 2, 3):
            re = re + (b[k] - b[8 - k]) * math.cos(math.pi * k * r / 8)
            im = im - (b[k] + b[8 - k]) * math.sin(math.pi * k * r / 8)
        y[r] = (re, im)
    return y


def whiten(x_ref, taps, tw_ref, fine_hi, fine_lo, tap_table, window, t_ref):
    for i in range(3):
        for j in range(2):
            rows, lanes = pl.ds(8 * i, 8), pl.ds(128 * j, 128)
            y = sixteen([x_ref[rows, pl.ds(256 * w + 128 * j, 128)] for w in range(16)])
            for r in range(16):
                re, im = y[min(r, 16 - r)]
                if r > 8:
                    im = -im
                if r:
                    c, s = tw_ref[pl.ds(r, 1), lanes], tw_ref[pl.ds(16 + r, 1), lanes]
                    re, im = re * c + im * s, im * c - re * s
                t_ref[pl.ds(24 * r + 8 * i, 8), lanes] = re
                t_ref[pl.ds(24 * r + 8 * i, 8), pl.ds(256 + 128 * j, 128)] = im
    hi, lo = halves(t_ref[...])
    fine = fine_hi[...]
    z = dot(hi, fine) + dot(lo, fine) + dot(hi, fine_lo[...])
    lane = lax.broadcasted_iota(jnp.int32, (24, 128), 1)
    ext = []
    for part in range(2):
        for j in range(2):
            tile = jnp.zeros((24, 128), F32)
            for r in range(8):
                piece = z[24 * (8 * j + r) : 24 * (8 * j + r) + 24, 128 * part : 128 * part + 128]
                tile = jnp.where(lane // 16 == r, piece, tile)
            ext.append(tile)
    padded = jnp.concatenate([taps, jnp.zeros((1, 64), F32)], axis=1)
    shifted = pltpu.roll(jnp.broadcast_to(padded, (128, 128)), 0, 1, stride=1, stride_axis=0)
    gains = dot(shifted, tap_table[...], precision=lax.Precision.HIGHEST)
    last = jnp.where(lane >= 64, x_ref[:, pl.ds(SAMPLES - 128, 128)], 0.0)
    cut = dot(last, gains, precision=lax.Precision.HIGHEST)
    h = [gains[0:1, 128 * k : 128 * k + 128] for k in range(4)]
    re = [h[j] * ext[j] - h[2 + j] * ext[2 + j] - cut[:, 128 * j : 128 * j + 128] for j in range(2)]
    im = [h[j] * ext[2 + j] + h[2 + j] * ext[j] - cut[:, 256 + 128 * j : 384 + 128 * j] for j in range(2)]
    power = jnp.concatenate([re[j] * re[j] + im[j] * im[j] for j in range(2)], axis=1)
    one = power.astype(BF16)
    rest = power - one.astype(F32)
    two = rest.astype(BF16)
    three = (rest - two.astype(F32)).astype(BF16)
    win = window[...]
    smooth = dot(one, win) + dot(two, win) + dot(three, win)
    scale = 1.0 / jnp.sqrt(smooth + 1e-06)
    r0, r1 = (re[j] * scale[:, 128 * j : 128 * j + 128] for j in range(2))
    i0, i1 = (im[j] * scale[:, 128 * j : 128 * j + 128] for j in range(2))
    slot = lane % 16
    band = (slot >= 2) & (slot < 14)

    def pack(a, b, c, d):
        return [
            jnp.where(band, t, pltpu.roll(d, s, 1)) for t, s in ((a, 12), (b, 8), (c, 4))
        ]

    return pack(r0, r1, i0, i1), pack(i0, i1, r0, r1)


def unpack(tiles, rows):
    slot = lax.broadcasted_iota(jnp.int32, (rows, 128), 1) % 16
    a, b, c = (pltpu.roll(t, s, 1) for t, s in zip(tiles, (116, 120, 124)))
    return jnp.where(slot < 6, a, jnp.where(slot < 10, b, c))


def mod(a, n):
    return lax.rem(a, jnp.int32(n))


def kernel(
    x_hbm, taps_ref, bins_hbm, tw_hbm, fhi_hbm, flo_hbm, tap_hbm, win_hbm, lhi_hbm, llo_hbm,
    out_ref,
    x_ref, tw_ref, fhi_ref, flo_ref, tap_ref, win_ref, lhi_ref, llo_ref, lev_ref, t_ref,
    zbuf, abuf, own_a, tiles, sib_tiles, wa_ref, hot, gath, x_acc, y_acc, part, r1, r2, r3,
    in_sem, lev_sem, z_send, z_recv, s_send, s_recv, p1_send, p1_recv, p2_send, p2_recv,
    r1_send, r1_recv, r2_send, r2_recv, r3_send, r3_recv,
):
    chan, place = lax.axis_index("chan"), lax.axis_index("bin")
    z, quad = lax.div(chan, jnp.int32(4)), mod(chan, 4)
    y_lo, core = lax.div(quad, jnp.int32(2)), mod(quad, 2)
    y_hi, x = lax.div(place, jnp.int32(4)), mod(place, 4)
    y = 2 * y_hi + y_lo
    upper = lax.div(z, jnp.int32(4))
    c = z + upper * (11 - 2 * z)
    me = 16 * y_lo + 8 * core + place

    def z_of(pos):
        return pos + lax.div(pos, jnp.int32(4)) * (11 - 2 * pos)

    def device(xx, yy, zz, cc):
        return (4 * zz + 2 * mod(yy, 2) + cc, 4 * lax.div(yy, jnp.int32(2)) + xx)

    loads = [
        pltpu.make_async_copy(src, dst, in_sem.at[i])
        for i, (src, dst) in enumerate(
            (
                (x_hbm, x_ref), (tw_hbm, tw_ref), (fhi_hbm, fhi_ref), (flo_hbm, flo_ref),
                (tap_hbm, tap_ref), (win_hbm, win_ref), (lhi_hbm, lhi_ref), (llo_hbm, llo_ref),
            )
        )
    ]
    for load in loads[:6]:
        load.start()
    levels = [z_of(mod(c + i, 8)) for i in range(5)]
    lev_loads = [
        pltpu.make_async_copy(
            bins_hbm.at[:, pl.ds(pl.multiple_of(levels[i] * LEVEL, 128), LEVEL)], lev_ref.at[i], lev_sem.at[i]
        )
        for i in range(5)
    ]
    for load in lev_loads:
        load.start()
    for load in loads[6:]:
        load.start()

    friends = [device(x, y, mod(z + d, 8), core) for d in range(1, 8)]
    friends += [device(mod(x + d, 4), y, z, core) for d in range(1, 4)]
    friends += [device(x, mod(y + d, 4), z, core) for d in range(1, 4)]
    friends += [device(mod(x + d, 4), mod(y + 2, 4), z, core) for d in range(1, 4)]
    other_quad = [mod(quad + d, 4) for d in range(1, 4)]
    pairs = [(4 * z + q, place) for q in other_quad]
    sibling = (chan + 1 - 2 * core, place)
    across = y + 1 - 2 * y_lo
    friends += [sibling, device(x, across, z, 1 - core)]
    barrier = pltpu.get_barrier_semaphore()
    for friend in friends:
        pl.semaphore_signal(barrier, inc=1, device_id=friend, device_id_type=MESH)

    def remote(src, dst, send, recv, to):
        return pltpu.make_async_remote_copy(
            src_ref=src, dst_ref=dst, send_sem=send, recv_sem=recv, device_id=to, device_id_type=MESH
        )

    for load in loads[:6]:
        load.wait()
    white, swapped = whiten(x_ref, taps_ref[...], tw_ref, fhi_ref, flo_ref, tap_ref, win_ref, t_ref)
    pad = jnp.zeros((8, 128), F32)
    for t in range(3):
        lanes = pl.ds(128 * t, 128)
        first = jnp.concatenate([white[t], pad], axis=0).astype(BF16)
        second = jnp.concatenate([swapped[t], pad], axis=0).astype(BF16)
        zbuf[0, :, lanes] = first
        own_a[0, :, lanes] = first
        own_a[1, :, lanes] = second
    pl.semaphore_wait(barrier, len(friends))

    sends = []

    def go(copy):
        copy.start()
        sends.append(copy)
        return copy

    z_copies = [
        go(remote(zbuf.at[0], zbuf.at[i], z_send.at[i - 1], z_recv.at[i - 1], device(x, y, z_of(mod(c + 8 - i, 8)), core)))
        for i in range(1, 5)
    ]
    a_copy = go(remote(own_a, abuf, s_send.at[0], s_recv.at[0], sibling))

    for load in lev_loads:
        load.wait()
    row = lax.broadcasted_iota(jnp.int32, (24, LEVEL), 0)
    col = lax.broadcasted_iota(jnp.int32, (24, LEVEL), 1)
    sign = 1 - 2 * upper
    after = (col - (24 * me + row)) * sign > 0
    lev_ref[0] = jnp.where(after, lev_ref[0], -1)
    half = (col >= LEVEL // 2).astype(jnp.int32)
    lev_ref[4] = jnp.where(mod(half + y_lo + upper, 2) == 0, lev_ref[4], -1)
    lane = lax.broadcasted_iota(jnp.int32, (24, 128), 1)
    for g in range(32):
        tile = jnp.full((24, 128), -1.0, F32)
        t0, off = divmod(24 * g, 128)
        for i in range(5):
            shift = (24 * i - off) % 128
            piece = pltpu.roll(lev_ref[i, :, pl.ds(128 * t0, 128)].astype(F32), shift, 1)
            if off > 104:
                more = pltpu.roll(lev_ref[i, :, pl.ds(128 * t0 + 128, 128)].astype(F32), shift, 1)
                piece = jnp.where(lane < 24 * i + 128 - off, piece, more)
            tile = jnp.where((lane >= 24 * i) & (lane < 24 * i + 24), piece, tile)
        tiles[g // 8 % 2, 8 * (g // 16) + g % 8] = tile
    b_copy = go(remote(tiles.at[1 - core], sib_tiles, s_send.at[1], s_recv.at[1], sibling))

    codes = lax.broadcasted_iota(jnp.int32, (64, 128), 0).astype(F32).astype(BF16)

    def place_of(d2, d1):
        xx = mod(x + core * d2 + (1 - core) * d1, 4)
        yy = mod(y + core * d1 + (1 - core) * d2, 4)
        return 8 * mod(yy, 2) + 4 * lax.div(yy, jnp.int32(2)) + xx

    def one_hots(source, base):
        def body(j, carry):
            at = place_of(lax.div(j, jnp.int32(4)), mod(j, 4))
            lanes = pl.ds(pl.multiple_of(128 * j, 128), 128)
            for a in range(24):
                bins = jnp.broadcast_to(source(at, a), (16, 128)).astype(BF16)
                for k in range(4):
                    hot[pl.ds(base + 64 * a + 16 * k, 16), lanes] = jnp.where(
                        bins == codes[16 * k : 16 * k + 16], jnp.ones((), BF16), jnp.zeros((), BF16)
                    )
            return carry

        lax.fori_loop(0, 16, body, 0)

    one_hots(lambda at, a: tiles[core, at, pl.ds(a, 1), :], 0)

    for copy in z_copies:
        copy.wait_recv()
    blocks = [zbuf[i, pl.ds(0, 32), :].astype(F32)[:24] for i in range(5)]
    gath[0, 0] = jnp.concatenate(blocks + [jnp.zeros((8, 384), F32)], axis=0).astype(BF16)

    def first(d):
        return device(mod(x + (1 - core) * d, 4), mod(y + core * d, 4), z, core)

    def second(d):
        return device(mod(x + core * d, 4), mod(y + (1 - core) * d, 4), z, core)

    order = (1, 3, 2)
    p1 = [go(remote(gath.at[0, 0], gath.at[0, 4 - d], p1_send.at[n], p1_recv.at[n], first(d))) for n, d in enumerate(order)]
    p2 = {}

    def forward(d1):
        for n, d in enumerate(order):
            p2[4 - d, d1] = go(
                remote(gath.at[0, d1], gath.at[4 - d, d1], p2_send.at[4 * n + d1], p2_recv.at[4 * n + d1], second(d))
            )

    forward(0)
    a_copy.wait_recv()
    b_copy.wait_recv()
    one_hots(lambda at, a: sib_tiles[at, pl.ds(a, 1), :], ROWS * NBINS)
    for i, block in enumerate((own_a, abuf)):
        for k in range(2):
            wa_ref[pl.ds(24 * i, 24), pl.ds(384 * k, 384)] = block[k].astype(F32)[:24]
    for n, d in enumerate(order):
        p1[n].wait_recv()
        forward(4 - d)

    x_acc[...] = jnp.zeros_like(x_acc)
    y_acc[...] = jnp.zeros_like(y_acc)

    def chunk(d2):
        weights = gath[d2].reshape(512, 384)

        def body(n, carry):
            rows = pl.ds(pl.multiple_of(512 * n, 512), 512)
            s = dot(hot[rows, pl.ds(512 * d2, 512)], weights)
            xs, ys = x_acc[...], y_acc[...]
            for a in range(8):
                w = wa_ref[pl.ds(8 * n + a, 1), :]
                piece = s[64 * a : 64 * a + 64]
                xs = xs + w[:, :384] * piece
                ys = ys + w[:, 384:] * piece
            x_acc[...] = xs
            y_acc[...] = ys
            return carry

        lax.fori_loop(0, 6, body, 0)

    chunk(0)
    for d in order:
        for d1 in range(4):
            p2[4 - d, d1].wait_recv()
        chunk(4 - d)

    xs = [x_acc[:, pl.ds(128 * t, 128)] for t in range(3)]
    ys = [y_acc[:, pl.ds(128 * t, 128)] for t in range(3)]
    signed = sign.astype(F32)
    sums = [xs[0] + xs[2], xs[1] + unpack(xs, 64), signed * (ys[0] - ys[2]), signed * (ys[1] - unpack(ys, 64))]
    for t in range(4):
        for k in range(8):
            part[k, :, pl.ds(128 * t, 128)] = sums[t][8 * k : 8 * k + 8]

    r1[place] = part[place]
    copies = []
    for d in range(1, 8):
        to = mod(place + d, 8)
        copies.append(go(remote(part.at[to], r1.at[place], r1_send.at[d - 1], r1_recv.at[d - 1], (chan, to))))
    for copy in copies:
        copy.wait_recv()

    def total(ref, n):
        value = ref[0]
        for i in range(1, n):
            value = value + ref[i]
        return value

    r2[quad] = total(r1, 8)
    copies = [
        go(remote(r2.at[quad], r2.at[quad], r2_send.at[d], r2_recv.at[d], pairs[d])) for d in range(3)
    ]
    for copy in copies:
        copy.wait_recv()
    r3[z] = total(r2, 4)
    copies = [
        go(remote(r3.at[z], r3.at[z], r3_send.at[d - 1], r3_recv.at[d - 1], (4 * mod(z + d, 8) + quad, place)))
        for d in range(1, 8)
    ]
    for load in loads[6:]:
        load.wait()
    for copy in copies:
        copy.wait_recv()
    hi, lo = halves(total(r3, 8))
    both = jnp.concatenate([hi.astype(F32), lo.astype(F32)], axis=0).astype(BF16)
    out = dot(both, lhi_ref[...]) + dot(both, llo_ref[...])
    out_ref[...] = out[:8] + out[8:]
    for copy in sends:
        copy.wait_send()


def solution(mesh):
    tables = make_tables()
    any_space = pl.BlockSpec(memory_space=pl.ANY)
    vmem = pl.BlockSpec(memory_space=pltpu.VMEM)
    dma = pltpu.SemaphoreType.DMA

    def step(traces, fir_taps, pair_bin):
        return pl.pallas_call(
            kernel,
            out_shape=jax.ShapeDtypeStruct((8, LAGS), F32),
            in_specs=[any_space, vmem, any_space] + [any_space] * len(tables),
            out_specs=vmem,
            scratch_shapes=[
                pltpu.VMEM((24, SAMPLES), F32),
                pltpu.VMEM((32, 256), F32),
                pltpu.VMEM((512, 256), BF16),
                pltpu.VMEM((512, 256), BF16),
                pltpu.VMEM((128, 512), F32),
                pltpu.VMEM((256, 256), BF16),
                pltpu.VMEM((512, 512), BF16),
                pltpu.VMEM((512, 512), BF16),
                pltpu.VMEM((5, 24, LEVEL), jnp.int32),
                pltpu.VMEM((384, 512), F32),
                pltpu.VMEM((5, 32, 384), BF16),
                pltpu.VMEM((2, 32, 384), BF16),
                pltpu.VMEM((2, 32, 384), BF16),
                pltpu.VMEM((2, 16, 24, 128), F32),
                pltpu.VMEM((16, 24, 128), F32),
                pltpu.VMEM((48, 768), F32),
                pltpu.VMEM((2 * ROWS * NBINS, 2048), BF16),
                pltpu.VMEM((4, 4, 128, 384), BF16),
                pltpu.VMEM((64, 384), F32),
                pltpu.VMEM((64, 384), F32),
                pltpu.VMEM((8, 8, 512), F32),
                pltpu.VMEM((8, 8, 512), F32),
                pltpu.VMEM((4, 8, 512), F32),
                pltpu.VMEM((8, 8, 512), F32),
                dma((8,)),
                dma((5,)),
                dma((4,)),
                dma((4,)),
                dma((2,)),
                dma((2,)),
                dma((3,)),
                dma((3,)),
                dma((12,)),
                dma((12,)),
                dma((7,)),
                dma((7,)),
                dma((3,)),
                dma((3,)),
                dma((7,)),
                dma((7,)),
            ],
            compiler_params=pltpu.CompilerParams(
                collective_id=0, has_side_effects=True, vmem_limit_bytes=56 * 2**20
            ),
            name="stack",
        )(traces, fir_taps.reshape(1, TAPS), pair_bin, *[jnp.asarray(t) for t in tables])

    return jax.shard_map(
        step,
        mesh=mesh,
        in_specs=(P(("chan", "bin"), None), P(), P(("chan", "bin"), None)),
        out_specs=P("bin", None),
        check_vma=False,
    )
```

```python
import math

import jax
import jax.numpy as jnp
import numpy as np
from jax import lax
from jax.experimental import pallas as pl
from jax.experimental.pallas import tpu as pltpu
from jax.sharding import PartitionSpec as P

SAMPLES = 4096
TAPS = 64
BAND_LO = 64
NF = 192
MARGIN = 32
LAGS = 512
NBINS = 64
ROWS = 24
LEVEL = 768
MESH = pl.DeviceIdType.MESH
F32 = jnp.float32
BF16 = jnp.bfloat16


def lane_freqs():
    lane = np.arange(128)
    return np.concatenate([16 * (lane % 16) + 8 * j + lane // 16 for j in range(2)])


HALF = [(dx, dy, dc) for dc in (0, 1) for dx, dy in ((1, 2), (3, 1), (3, 3), (2, 3), (1, 0), (0, 1))]
HALF += [(dx, dy, dc) for dx, dy, dc in np.ndindex(3, 3, 2) if dx != 1 and dy != 1][::-1]
TIES = 12
DEPTH = 512


def geometry():
    table = np.zeros((8, DEPTH), np.int32)
    table[3], table[4] = -4096, 2
    for slot, h in enumerate(HALF):
        at = slice(ROWS * slot, ROWS * slot + ROWS)
        table[:3, at] = np.array(h)[:, None]
        table[3, at] = np.arange(ROWS)
        table[4, at] = slot >= TIES
    return table


def make_tables():
    e = lane_freqs()
    u = np.arange(256)
    ang = 2 * math.pi / SAMPLES * ((u[None, :] * np.arange(16)[:, None]) % SAMPLES)
    twiddle = np.concatenate([np.cos(ang), np.sin(ang)], 0).astype(np.float32)
    p = 2 + np.arange(128) % 16
    ang = 2 * math.pi / 256 * ((u[:, None] * p[None, :]) % 256)
    c, s = np.cos(ang), np.sin(ang)
    fine = np.concatenate([np.concatenate([c, -s], 1), np.concatenate([s, c], 1)], 0)
    ang = 2 * math.pi / SAMPLES * ((np.arange(128)[:, None] * (32 + e)[None, :]) % SAMPLES)
    taps = np.concatenate([np.cos(ang), -np.sin(ang)], 1)
    taps[TAPS:] = 0.0
    window = ((e[:, None] >= e[None, :] - MARGIN) & (e[:, None] < e[None, :] + MARGIN)) / (2.0 * MARGIN)
    f = e - MARGIN
    ok = (f >= 0) & (f < NF)
    phase = ((BAND_LO + np.where(ok, f, 0))[:, None] * (np.arange(LAGS) - LAGS // 2)[None, :]) % SAMPLES
    ang = 2 * math.pi / SAMPLES * phase
    lag = np.concatenate([np.cos(ang), -np.sin(ang)], 0) * (2.0 / SAMPLES) * np.concatenate([ok, ok])[:, None]
    return [t.astype(np.float32) for t in (twiddle, fine, taps, window, lag)] + [geometry()]


def dot(a, b, **kw):
    return jnp.dot(a, b, preferred_element_type=F32, **kw)


def halves(a):
    hi = a.astype(BF16)
    return hi, (a - hi.astype(F32)).astype(BF16)


def sixteen(x):
    root = math.sqrt(0.5)
    a = [x[k] + x[k + 8] for k in range(8)]
    b = [x[k] - x[k + 8] for k in range(8)]
    c = [a[k] + a[k + 4] for k in range(4)]
    d = [a[k] - a[k + 4] for k in range(4)]
    y = [None] * 9
    zero = jnp.zeros_like(x[0])
    even, odd = c[0] + c[2], c[1] + c[3]
    y[0] = (even + odd, zero)
    y[8] = (even - odd, zero)
    y[4] = (c[0] - c[2], c[3] - c[1])
    m, n = (d[1] - d[3]) * root, (d[1] + d[3]) * root
    y[2] = (d[0] + m, -(n + d[2]))
    y[6] = (d[0] - m, d[2] - n)
    for r in (1, 3, 5, 7):
        re, im = b[0], b[4] * (-1.0 if r % 4 == 1 else 1.0)
        for k in (1, 2, 3):
            re = re + (b[k] - b[8 - k]) * math.cos(math.pi * k * r / 8)
            im = im - (b[k] + b[8 - k]) * math.sin(math.pi * k * r / 8)
        y[r] = (re, im)
    return y


def whiten(x_ref, taps, tw_ref, fine_ref, tap_table, window, t_ref):
    def body(i, carry):
        rows = pl.ds(pl.multiple_of(8 * i, 8), 8)
        for j in range(2):
            lanes = pl.ds(128 * j, 128)
            y = sixteen([x_ref[rows, pl.ds(256 * w + 128 * j, 128)] for w in range(16)])
            for r in range(16):
                re, im = y[min(r, 16 - r)]
                if r > 8:
                    im = -im
                if r:
                    c, s = tw_ref[pl.ds(r, 1), lanes], tw_ref[pl.ds(16 + r, 1), lanes]
                    re, im = re * c + im * s, im * c - re * s
                at = pl.ds(pl.multiple_of(24 * r + 8 * i, 8), 8)
                t_ref[at, lanes] = re
                t_ref[at, pl.ds(256 + 128 * j, 128)] = im
        return carry

    lax.fori_loop(0, 3, body, 0)
    hi, lo = halves(t_ref[...])
    fine, fine_lo = halves(fine_ref[...])
    z = dot(hi, fine) + dot(lo, fine) + dot(hi, fine_lo)
    lane = lax.broadcasted_iota(jnp.int32, (24, 128), 1)
    ext = []
    for part in range(2):
        for j in range(2):
            tile = jnp.zeros((24, 128), F32)
            for r in range(8):
                piece = z[24 * (8 * j + r) : 24 * (8 * j + r) + 24, 128 * part : 128 * part + 128]
                tile = jnp.where(lane // 16 == r, piece, tile)
            ext.append(tile)
    padded = jnp.concatenate([taps, jnp.zeros((1, 64), F32)], axis=1)
    shifted = pltpu.roll(jnp.broadcast_to(padded, (128, 128)), 0, 1, stride=1, stride_axis=0)
    gains = dot(shifted, tap_table[...], precision=lax.Precision.HIGHEST)
    last = jnp.where(lane >= 64, x_ref[:, pl.ds(SAMPLES - 128, 128)], 0.0)
    cut = dot(last, gains, precision=lax.Precision.HIGHEST)
    h = [gains[0:1, 128 * k : 128 * k + 128] for k in range(4)]
    re = [h[j] * ext[j] - h[2 + j] * ext[2 + j] - cut[:, 128 * j : 128 * j + 128] for j in range(2)]
    im = [h[j] * ext[2 + j] + h[2 + j] * ext[j] - cut[:, 256 + 128 * j : 384 + 128 * j] for j in range(2)]
    power = jnp.concatenate([re[j] * re[j] + im[j] * im[j] for j in range(2)], axis=1)
    one = power.astype(BF16)
    rest = power - one.astype(F32)
    two = rest.astype(BF16)
    three = (rest - two.astype(F32)).astype(BF16)
    win = window[...].astype(BF16)
    smooth = dot(one, win) + dot(two, win) + dot(three, win)
    scale = 1.0 / jnp.sqrt(smooth + 1e-06)
    r0, r1 = (re[j] * scale[:, 128 * j : 128 * j + 128] for j in range(2))
    i0, i1 = (im[j] * scale[:, 128 * j : 128 * j + 128] for j in range(2))
    slot = lane % 16
    band = (slot >= 2) & (slot < 14)

    def pack(a, b, c, d):
        return [
            jnp.where(band, t, pltpu.roll(d, s, 1)) for t, s in ((a, 12), (b, 8), (c, 4))
        ]

    return pack(r0, r1, i0, i1)


def swap(tiles):
    a, b, c = tiles
    slot = lax.broadcasted_iota(jnp.int32, (ROWS, 128), 1) % 16
    band = (slot >= 2) & (slot < 14)
    full = (c, unpack(tiles, ROWS), a)
    return [jnp.where(band, t, pltpu.roll(b, s, 1)) for t, s in zip(full, (12, 8, 4))]


def unpack(tiles, rows):
    slot = lax.broadcasted_iota(jnp.int32, (rows, 128), 1) % 16
    a, b, c = (pltpu.roll(t, s, 1) for t, s in zip(tiles, (116, 120, 124)))
    return jnp.where(slot < 6, a, jnp.where(slot < 10, b, c))


def mod(a, n):
    return lax.rem(a, jnp.int32(n))


def fold(rows, width):
    parts = [rows[16:, i : i + width] for i in range(0, rows.shape[1], width)]
    if parts[1].shape[1] < width:
        parts[1] = jnp.concatenate([parts[1], jnp.zeros((8, width - parts[1].shape[1]), F32)], axis=1)
    return jnp.concatenate([rows[:16], jnp.concatenate(parts, axis=0)], axis=1).astype(BF16)


def unfold(block, cols, width):
    wide = block.astype(F32)
    tail = [wide[:8, cols:], wide[8:, cols : 2 * cols - width]]
    return jnp.concatenate([wide[:, :cols], jnp.concatenate(tail, axis=1)], axis=0)


def kernel(
    x_hbm, taps_ref, bins_hbm, tw_hbm, fine_hbm, tap_hbm, win_hbm, lag_hbm, geo_hbm,
    out_ref,
    x_ref, tw_ref, fine_ref, tap_ref, win_ref, lag_ref, geo_ref, lev_ref, t_ref, lhi_ref, llo_ref,
    mine, bbuf, abuf, bsend, brecv, codes_ref, wa_ref, hot0, hot1, bmat, s0, s1, x_acc, y_acc, part, r1, r2, r3,
    in_sem, lev_sem, b_send, b_recv, a_send, a_recv, c_send, c_recv,
    r1_send, r1_recv, r2_send, r2_recv, r3_send, r3_recv,
):
    chan, place = lax.axis_index("chan"), lax.axis_index("bin")
    z, quad = lax.div(chan, jnp.int32(4)), mod(chan, 4)
    y_lo, core = lax.div(quad, jnp.int32(2)), mod(quad, 2)
    y_hi, x = lax.div(place, jnp.int32(4)), mod(place, 4)
    y = 2 * y_hi + y_lo
    me = 16 * y_lo + 8 * core + place

    def device(dx, dy, dz, dc):
        xx, yy, zz, cc = mod(x + dx, 4), mod(y + dy, 4), mod(z + dz, 8), mod(core + dc, 2)
        return (4 * zz + 2 * mod(yy, 2) + cc, 4 * lax.div(yy, jnp.int32(2)) + xx)

    lev_loads = [
        pltpu.make_async_copy(
            bins_hbm.at[:, pl.ds(pl.multiple_of(mod(z + d, 8) * LEVEL, 128), LEVEL)], lev_ref.at[d], lev_sem.at[d]
        )
        for d in range(8)
    ]
    loads = [
        pltpu.make_async_copy(src, dst, in_sem.at[i])
        for i, (src, dst) in enumerate(
            (
                (x_hbm, x_ref), (tw_hbm, tw_ref), (fine_hbm, fine_ref), (tap_hbm, tap_ref), (win_hbm, win_ref),
                (geo_hbm, geo_ref), (lag_hbm, lag_ref),
            )
        )
    ]
    for load in loads[:5] + lev_loads + loads[5:]:
        load.start()

    plane = [h for h in np.ndindex(4, 4, 2) if any(h)]
    plane.sort(key=lambda h: -(min(h[0], 4 - h[0]) + min(h[1], 4 - h[1])))
    plane = [tuple(map(int, h)) for h in plane]
    friends = [device(dx, dy, 0, dc) for dx, dy, dc in plane] + [device(0, 0, d, 0) for d in (4, 3, 5, 2, 6, 1, 7)]
    barrier = pltpu.get_barrier_semaphore()
    for friend in friends:
        pl.semaphore_signal(barrier, inc=1, device_id=friend, device_id_type=MESH)

    def remote(src, dst, send, recv, to):
        return pltpu.make_async_remote_copy(
            src_ref=src, dst_ref=dst, send_sem=send, recv_sem=recv, device_id=to, device_id_type=MESH
        )

    sibling = device(0, 0, 0, 1)
    for load in loads[:5]:
        load.wait()
    white = whiten(x_ref, taps_ref[...], tw_ref, fine_ref, tap_ref, win_ref, t_ref)
    mine[...] = fold(jnp.concatenate(white, axis=1), 256)
    pl.semaphore_wait(barrier, len(friends))

    far_first = sorted(range(len(HALF) - 1), key=lambda n: -sum(min(v, 4 - v) for v in HALF[n][:2]))
    for n in far_first:
        h = HALF[n]
        remote(mine, bbuf.at[n], b_send, b_recv, device(4 - h[0], 4 - h[1], 0, h[2])).start()
    order = (1, 7, 2, 6, 3, 5, 4)
    slot_of = {d: n for n, d in enumerate(order)}
    for d in order:
        n = slot_of[8 - d]
        remote(mine, abuf.at[n], a_send, a_recv.at[n], device(0, 0, d, 0)).start()

    loads[5].wait()
    dx, dy, dc = (geo_ref[pl.ds(i, 1), :] for i in range(3))
    kind = geo_ref[pl.ds(4, 1), :]
    xx, yy, cc = (x + dx) & 3, (y + dy) & 3, (core + dc) & 1
    source = 24 * (16 * (yy & 1) + 8 * cc + 4 * (yy >> 1) + xx) + geo_ref[pl.ds(3, 1), :]
    pick = (lax.broadcasted_iota(jnp.int32, (LEVEL, DEPTH), 0) == source).astype(F32).astype(BF16)
    for load in lev_loads:
        load.wait()
    picked = dot(lev_ref[...].reshape(8 * ROWS, LEVEL).astype(F32).astype(BF16), pick)
    for d in order:
        above = (mod(z + d, 8) > z).astype(jnp.int32)
        keep = jnp.broadcast_to(kind <= above, (ROWS, DEPTH))
        bsend[d - 1] = fold(jnp.where(keep, picked[ROWS * d : ROWS * d + ROWS], -1.0), 256)
    for d in order:
        n = slot_of[8 - d]
        remote(bsend.at[d - 1], brecv.at[n], c_send, c_recv.at[n], device(0, 0, d, 0)).start()
    own = 24 * me + lax.broadcasted_iota(jnp.int32, (ROWS, DEPTH), 0)
    codes_ref[pl.ds(0, ROWS), :] = jnp.where((kind < 2) & (source > own), picked[:ROWS], -1.0)
    codes_ref[pl.ds(ROWS, ROWS), :] = jnp.where((kind < 1) & (source < own), picked[:ROWS], -1.0)

    def set_rows(slot, rows, sign):
        tiles = [rows[:, 128 * t : 128 * t + 128] for t in range(3)]
        at = pl.ds(pl.multiple_of(ROWS * slot, 8), ROWS)
        for t, (one, two) in enumerate(zip(tiles, swap(tiles))):
            wa_ref[at, pl.ds(128 * t, 128)] = one
            wa_ref[at, pl.ds(384 + 128 * t, 128)] = two * sign

    def block_of(ref):
        return unfold(ref[...], 384, 256)

    bins = lax.broadcasted_iota(jnp.int32, (64, 128), 0).astype(F32).astype(BF16)

    def one_hots(out, slot, part):
        codes = codes_ref[pl.ds(pl.multiple_of(ROWS * slot, 8), ROWS), :]
        for a in range(12):
            row = codes[12 * part + a : 12 * part + a + 1]
            for t in range(4):
                lanes = pl.ds(128 * t, 128)
                code = jnp.broadcast_to(row[:, 128 * t : 128 * t + 128], (16, 128)).astype(BF16)
                for k in range(4):
                    out[pl.ds(64 * a + 16 * k, 16), lanes] = jnp.where(
                        code == bins[16 * k : 16 * k + 16], jnp.ones((), BF16), jnp.zeros((), BF16)
                    )

    def take(slot, part, ref):
        rows = pl.ds(pl.multiple_of(ROWS * slot, 8), ROWS)
        for t in range(3):
            lanes, more = pl.ds(128 * t, 128), pl.ds(384 + 128 * t, 128)
            w, v = wa_ref[rows, lanes], wa_ref[rows, more]
            xs, ys = x_acc[:, lanes], y_acc[:, lanes]
            for a in range(12):
                at = 12 * part + a
                piece = ref[pl.ds(64 * a, 64), lanes]
                xs = xs + w[at : at + 1] * piece
                ys = ys + v[at : at + 1] * piece
            x_acc[:, lanes] = xs
            y_acc[:, lanes] = ys

    one_hots(hot0, 0, 0)
    rows = block_of(mine)
    set_rows(0, rows, 1.0)
    set_rows(1, rows, -1.0)
    x_acc[...] = jnp.zeros_like(x_acc)
    y_acc[...] = jnp.zeros_like(y_acc)
    s1[...] = jnp.zeros_like(s1)
    loads[6].wait()
    lag_hi, lag_lo = halves(lag_ref[...])
    lhi_ref[...] = lag_hi
    llo_ref[...] = lag_lo
    blocks = len(HALF)
    bmat[pl.ds(ROWS * blocks, DEPTH - ROWS * blocks), :] = jnp.zeros((DEPTH - ROWS * blocks, 384), BF16)
    remote(bbuf, bbuf, b_send, b_recv, sibling).wait_recv()
    for n in range(0, blocks, 2):
        two = [block_of(bbuf.at[m]) if m < blocks - 1 else rows for m in (n, n + 1)]
        bmat[pl.ds(ROWS * n, 2 * ROWS), :] = jnp.concatenate(two, axis=0).astype(BF16)

    def body(slot, carry):
        after = slot + 1

        @pl.when((slot > 0) & (slot < 8))
        def _():
            n = slot - 1
            remote(brecv.at[n], brecv.at[n], c_send, c_recv.at[n], sibling).wait_recv()
            remote(abuf.at[n], abuf.at[n], a_send, a_recv.at[n], sibling).wait_recv()
            codes_ref[pl.ds(pl.multiple_of(ROWS * after, 8), ROWS), :] = unfold(brecv[n], 512, 256)
            k = lax.div(after, jnp.int32(2))
            d = k + mod(after, 2) * (8 - 2 * k)
            below = (mod(z + d, 8) < z).astype(F32)
            set_rows(after, block_of(abuf.at[n]), 2.0 * below - 1.0)

        s0[...] = dot(hot0[...], bmat[...])
        one_hots(hot1, slot, 1)
        take(jnp.maximum(slot - 1, 0), 1, s1)
        s1[...] = dot(hot1[...], bmat[...])
        one_hots(hot0, jnp.minimum(after, 8), 0)
        take(slot, 0, s0)
        return carry

    lax.fori_loop(0, 9, body, 0)
    take(8, 1, s1)

    xs = [x_acc[:, pl.ds(128 * t, 128)] for t in range(3)]
    ys = [y_acc[:, pl.ds(128 * t, 128)] for t in range(3)]
    sums = [xs[0] + xs[2], xs[1] + unpack(xs, 64), ys[0] - ys[2], ys[1] - unpack(ys, 64)]
    for t in range(4):
        for k in range(8):
            part[k, t] = sums[t][8 * k : 8 * k + 8]

    at = 4 * place + quad
    r1[at] = part[place, quad]
    for n, (dx, dy, dc) in enumerate(plane):
        to = device(dx, dy, 0, dc)
        remote(part.at[to[1], mod(to[0], 4)], r1.at[at], r1_send, r1_recv, to).start()
    remote(r1.at[pl.ds(0, 31)], r1.at[pl.ds(0, 31)], r1_send, r1_recv, sibling).wait_recv()

    def total(ref, n):
        values = [ref[i] for i in range(n)]
        while len(values) > 1:
            values = [a + b for a, b in zip(values[::2], values[1::2])]
        return values[0]

    r2[z] = total(r1, 32)
    for d in (4, 3, 5, 2, 6, 1, 7):
        remote(r2.at[z], r2.at[z], r2_send, r2_recv, device(0, 0, d, 0)).start()
    remote(r2.at[pl.ds(0, 7)], r2.at[pl.ds(0, 7)], r2_send, r2_recv, sibling).wait_recv()
    r3[quad] = total(r2, 8)
    for d in range(1, 4):
        to = (4 * z + mod(quad + d, 4), place)
        remote(r3.at[quad], r3.at[quad], r3_send, r3_recv, to).start()
    remote(r3.at[pl.ds(0, 3)], r3.at[pl.ds(0, 3)], r3_send, r3_recv, sibling).wait_recv()
    hi, lo = halves(jnp.concatenate([r3[t] for t in range(4)], axis=1))
    both = jnp.concatenate([hi.astype(F32), lo.astype(F32)], axis=0).astype(BF16)
    out = dot(both, lhi_ref[...]) + dot(both, llo_ref[...])
    out_ref[...] = out[:8] + out[8:]
    for src, send, recv in (
        (bbuf, b_send, b_recv), (abuf, a_send, a_recv.at[0]), (bsend, c_send, c_recv.at[0]),
        (r1.at[pl.ds(0, 31)], r1_send, r1_recv), (r2.at[pl.ds(0, 7)], r2_send, r2_recv), (r3.at[pl.ds(0, 3)], r3_send, r3_recv),
    ):
        remote(src, src, send, recv, sibling).wait_send()


def solution(mesh):
    tables = make_tables()
    any_space = pl.BlockSpec(memory_space=pl.ANY)
    vmem = pl.BlockSpec(memory_space=pltpu.VMEM)
    dma = pltpu.SemaphoreType.DMA
    n = len(HALF)

    def step(traces, fir_taps, pair_bin):
        return pl.pallas_call(
            kernel,
            out_shape=jax.ShapeDtypeStruct((8, LAGS), F32),
            in_specs=[any_space, vmem, any_space] + [any_space] * len(tables),
            out_specs=vmem,
            scratch_shapes=[
                pltpu.VMEM((ROWS, SAMPLES), F32),
                *[pltpu.VMEM(t.shape, t.dtype) for t in tables],
                pltpu.VMEM((8, ROWS, LEVEL), jnp.int32),
                pltpu.VMEM((16 * ROWS, 512), F32),
                pltpu.VMEM((512, 512), BF16),
                pltpu.VMEM((512, 512), BF16),
                pltpu.VMEM((16, 640), BF16),
                pltpu.VMEM((n - 1, 16, 640), BF16),
                pltpu.VMEM((7, 16, 640), BF16),
                pltpu.VMEM((7, 16, 768), BF16),
                pltpu.VMEM((7, 16, 768), BF16),
                pltpu.VMEM((9 * ROWS, DEPTH), F32),
                pltpu.VMEM((9 * ROWS, 768), F32),
                pltpu.VMEM((12 * NBINS, DEPTH), BF16),
                pltpu.VMEM((12 * NBINS, DEPTH), BF16),
                pltpu.VMEM((DEPTH, 384), BF16),
                pltpu.VMEM((12 * NBINS, 384), F32),
                pltpu.VMEM((12 * NBINS, 384), F32),
                pltpu.VMEM((64, 384), F32),
                pltpu.VMEM((64, 384), F32),
                pltpu.VMEM((8, 4, 8, 128), F32),
                pltpu.VMEM((32, 8, 128), F32),
                pltpu.VMEM((8, 8, 128), F32),
                pltpu.VMEM((4, 8, 128), F32),
                dma((7,)),
                dma((8,)),
                dma(()),
                dma(()),
                dma(()),
                dma((7,)),
                dma(()),
                dma((7,)),
                dma(()),
                dma(()),
                dma(()),
                dma(()),
                dma(()),
                dma(()),
            ],
            compiler_params=pltpu.CompilerParams(
                collective_id=0, has_side_effects=True, vmem_limit_bytes=56 * 2**20
            ),
            name="stack",
        )(traces, fir_taps.reshape(1, TAPS), pair_bin, *[jnp.asarray(t) for t in tables])

    return jax.shard_map(
        step,
        mesh=mesh,
        in_specs=(P(("chan", "bin"), None), P(), P(("chan", "bin"), None)),
        out_specs=P("bin", None),
        check_vma=False,
    )
```

```python
import math

import jax
import jax.numpy as jnp
import numpy as np
from jax import lax
from jax.experimental import pallas as pl
from jax.experimental.pallas import tpu as pltpu
from jax.sharding import PartitionSpec as P

SAMPLES = 4096
TAPS = 64
BAND_LO = 64
NF = 192
MARGIN = 32
LAGS = 512
NBINS = 64
ROWS = 24
LEVEL = 768
MESH = pl.DeviceIdType.MESH
F32 = jnp.float32
BF16 = jnp.bfloat16


def lane_freqs():
    lane = np.arange(128)
    return np.concatenate([16 * (lane % 16) + 8 * j + lane // 16 for j in range(2)])


HALF = [(2, 2), (1, 2), (2, 3), (3, 1), (3, 3), (2, 0), (0, 2), (1, 0), (0, 1), (0, 0)]
FAR = 3
DEPTH = 512


def geometry():
    table = np.zeros((8, DEPTH), np.int32)
    table[3], table[4] = -4096, 2
    for slot in range(2 * len(HALF)):
        at = slice(ROWS * slot, ROWS * slot + ROWS)
        dc, n = divmod(slot, len(HALF))
        table[:3, at] = np.array((*HALF[n], dc))[:, None]
        table[3, at] = np.arange(ROWS)
        table[4, at] = not any(v % 2 for v in HALF[n])
    return table


def make_tables():
    e = lane_freqs()
    u = np.arange(256)
    ang = 2 * math.pi / SAMPLES * ((u[None, :] * np.arange(16)[:, None]) % SAMPLES)
    twiddle = np.concatenate([np.cos(ang), np.sin(ang)], 0).astype(np.float32)
    p = 2 + np.arange(128) % 16
    ang = 2 * math.pi / 256 * ((u[:, None] * p[None, :]) % 256)
    c, s = np.cos(ang), np.sin(ang)
    fine = np.concatenate([c, s], 1)
    ang = 2 * math.pi / SAMPLES * ((np.arange(TAPS)[:, None] * (32 + e)[None, :]) % SAMPLES)
    taps = np.concatenate([np.cos(ang), -np.sin(ang)], 1)
    f = e - MARGIN
    ok = (f >= 0) & (f < NF)
    phase = ((BAND_LO + np.where(ok, f, 0))[:, None] * (np.arange(LAGS) - LAGS // 2)[None, :]) % SAMPLES
    ang = 2 * math.pi / SAMPLES * phase
    lag = np.concatenate([np.cos(ang), -np.sin(ang)], 0) * (2.0 / SAMPLES) * np.concatenate([ok, ok])[:, None]
    return [t.astype(np.float32) for t in (twiddle, fine, taps, lag)] + [geometry()]


def dot(a, b, **kw):
    return jnp.dot(a, b, preferred_element_type=F32, **kw)


def halves(a):
    hi = a.astype(BF16)
    return hi, (a - hi.astype(F32)).astype(BF16)


def sixteen(x):
    root = math.sqrt(0.5)
    a = [x[k] + x[k + 8] for k in range(8)]
    b = [x[k] - x[k + 8] for k in range(8)]
    c = [a[k] + a[k + 4] for k in range(4)]
    d = [a[k] - a[k + 4] for k in range(4)]
    y = [None] * 9
    zero = jnp.zeros_like(x[0])
    even, odd = c[0] + c[2], c[1] + c[3]
    y[0] = (even + odd, zero)
    y[8] = (even - odd, zero)
    y[4] = (c[0] - c[2], c[3] - c[1])
    m, n = (d[1] - d[3]) * root, (d[1] + d[3]) * root
    y[2] = (d[0] + m, -(n + d[2]))
    y[6] = (d[0] - m, d[2] - n)
    for r in (1, 3, 5, 7):
        re, im = b[0], b[4] * (-1.0 if r % 4 == 1 else 1.0)
        for k in (1, 2, 3):
            re = re + (b[k] - b[8 - k]) * math.cos(math.pi * k * r / 8)
            im = im - (b[k] + b[8 - k]) * math.sin(math.pi * k * r / 8)
        y[r] = (re, im)
    return y


def freq_of(shape, axis):
    i = lax.broadcasted_iota(jnp.int32, shape, axis)
    return 16 * (i & 15) + 8 * (i >> 7) + ((i >> 4) & 7)


def whiten(x_ref, taps, tw_ref, fine_ref, tap_table, hi_ref, lo_ref, loads):
    padded = jnp.concatenate([taps, jnp.zeros((1, 64), F32)], axis=1)
    shifted = pltpu.roll(jnp.broadcast_to(padded, (128, 128)), 0, 1, stride=1, stride_axis=0)
    target = freq_of((256, 256), 1)
    apart = freq_of((256, 256), 0) - target
    win = jnp.where((apart >= -MARGIN) & (apart < MARGIN), 0.5 / MARGIN, 0.0).astype(BF16)
    loads["taps"].wait()
    gains = dot(shifted[:, :TAPS], tap_table[...], precision=lax.Precision.HIGHEST)
    loads["x"].wait()
    loads["tw"].wait()

    def body(i, carry):
        rows = pl.ds(pl.multiple_of(8 * i, 8), 8)
        for j in range(2):
            lanes = pl.ds(128 * j, 128)
            y = sixteen([x_ref[rows, pl.ds(256 * w + 128 * j, 128)] for w in range(16)])
            parts = []
            for r in range(16):
                re, im = y[min(r, 16 - r)]
                if r > 8:
                    im = -im
                if r:
                    c, s = tw_ref[pl.ds(r, 1), lanes], tw_ref[pl.ds(16 + r, 1), lanes]
                    re, im = re * c + im * s, im * c - re * s
                parts.append((re, im))
            for r in range(0, 16, 2):
                at = pl.ds(pl.multiple_of(128 * i + 8 * r, 16), 16)
                for k in range(2):
                    hi, lo = halves(jnp.concatenate([parts[r][k], parts[r + 1][k]], axis=0))
                    hi_ref[at, pl.ds(256 * k + 128 * j, 128)] = hi
                    lo_ref[at, pl.ds(256 * k + 128 * j, 128)] = lo
        return carry

    lax.fori_loop(0, 3, body, 0)
    loads["fine"].wait()
    both = fine_ref[...]
    c, s = halves(both[:, :128]), halves(both[:, 128:])
    fine = [jnp.concatenate([jnp.concatenate([c[k], -s[k]], 1), jnp.concatenate([s[k], c[k]], 1)], 0) for k in range(2)]
    left = jnp.concatenate([hi_ref[...], lo_ref[...], hi_ref[...]], axis=1)
    z = dot(left, jnp.concatenate([fine[0], fine[0], fine[1]], axis=0))
    lane = lax.broadcasted_iota(jnp.int32, (24, 128), 1)
    ext = []
    for part in range(2):
        for j in range(2):
            tile = jnp.zeros((24, 128), F32)
            for r in range(8):
                at = 8 * (8 * j + r)
                piece = jnp.concatenate([z[128 * i + at : 128 * i + at + 8, 128 * part : 128 * part + 128] for i in range(3)], 0)
                tile = jnp.where(lane // 16 == r, piece, tile)
            ext.append(tile)
    last = jnp.where(lane >= 64, x_ref[:, pl.ds(SAMPLES - 128, 128)], 0.0)
    cut = dot(last, gains, precision=lax.Precision.HIGHEST)
    h = [gains[0:1, 128 * k : 128 * k + 128] for k in range(4)]
    re = [h[j] * ext[j] - h[2 + j] * ext[2 + j] - cut[:, 128 * j : 128 * j + 128] for j in range(2)]
    im = [h[j] * ext[2 + j] + h[2 + j] * ext[j] - cut[:, 256 + 128 * j : 384 + 128 * j] for j in range(2)]
    power = jnp.concatenate([re[j] * re[j] + im[j] * im[j] for j in range(2)], axis=1)
    one = power.astype(BF16)
    rest = power - one.astype(F32)
    two = rest.astype(BF16)
    three = (rest - two.astype(F32)).astype(BF16)
    smooth = dot(one, win) + dot(two, win) + dot(three, win)
    scale = 1.0 / jnp.sqrt(smooth + 1e-06)
    r0, r1 = (re[j] * scale[:, 128 * j : 128 * j + 128] for j in range(2))
    i0, i1 = (im[j] * scale[:, 128 * j : 128 * j + 128] for j in range(2))
    slot = lane % 16
    band = (slot >= 2) & (slot < 14)

    def pack(a, b, c, d):
        return [
            jnp.where(band, t, pltpu.roll(d, s, 1)) for t, s in ((a, 12), (b, 8), (c, 4))
        ]

    return pack(r0, r1, i0, i1)


def swap(tiles):
    a, b, c = tiles
    slot = lax.broadcasted_iota(jnp.int32, (ROWS, 128), 1) % 16
    band = (slot >= 2) & (slot < 14)
    full = (c, unpack(tiles, ROWS), a)
    return [jnp.where(band, t, pltpu.roll(b, s, 1)) for t, s in zip(full, (12, 8, 4))]


def unpack(tiles, rows):
    slot = lax.broadcasted_iota(jnp.int32, (rows, 128), 1) % 16
    a, b, c = (pltpu.roll(t, s, 1) for t, s in zip(tiles, (116, 120, 124)))
    return jnp.where(slot < 6, a, jnp.where(slot < 10, b, c))


def mod(a, n):
    return lax.rem(a, jnp.int32(n))


def fold(rows, width):
    parts = [rows[16:, i : i + width] for i in range(0, rows.shape[1], width)]
    if parts[1].shape[1] < width:
        parts[1] = jnp.concatenate([parts[1], jnp.zeros((8, width - parts[1].shape[1]), F32)], axis=1)
    return jnp.concatenate([rows[:16], jnp.concatenate(parts, axis=0)], axis=1).astype(BF16)


def unfold(block, cols, width):
    wide = block.astype(F32)
    tail = [wide[:8, cols:], wide[8:, cols : 2 * cols - width]]
    return jnp.concatenate([wide[:, :cols], jnp.concatenate(tail, axis=1)], axis=0)


def kernel(
    x_hbm, taps_ref, bins_hbm, tw_hbm, fine_hbm, tap_hbm, lag_hbm, geo_hbm,
    out_ref,
    x_ref, tw_ref, fine_ref, tap_ref, lag_ref, geo_ref, lev_ref, pick_ref, hi_ref, lo_ref, lhi_ref, llo_ref,
    bbuf, abuf, bsend, brecv, codes_ref, wa_ref, hot0, hot1, bmat, s0, s1, x_acc, y_acc, part, r1, r2, r3,
    in_sem, lev_sem, b_send, b_recv, s_send, s_recv, a_send, a_recv, c_send, c_recv,
    r1_send, r1_recv, r2_send, r2_recv, r3_send, r3_recv,
):
    chan, place = lax.axis_index("chan"), lax.axis_index("bin")
    z, quad = lax.div(chan, jnp.int32(4)), mod(chan, 4)
    y_lo, core = lax.div(quad, jnp.int32(2)), mod(quad, 2)
    y_hi, x = lax.div(place, jnp.int32(4)), mod(place, 4)
    y = 2 * y_hi + y_lo
    me = 16 * y_lo + 8 * core + place

    def device(dx, dy, dz, dc):
        xx, yy, zz, cc = mod(x + dx, 4), mod(y + dy, 4), mod(z + dz, 8), mod(core + dc, 2)
        return (4 * zz + 2 * mod(yy, 2) + cc, 4 * lax.div(yy, jnp.int32(2)) + xx)

    lev_loads = [
        pltpu.make_async_copy(
            bins_hbm.at[:, pl.ds(pl.multiple_of(mod(z + d, 8) * LEVEL, 128), LEVEL)], lev_ref.at[d], lev_sem.at[d]
        )
        for d in range(8)
    ]
    copies = dict(
        taps=(tap_hbm, tap_ref), x=(x_hbm, x_ref), tw=(tw_hbm, tw_ref), fine=(fine_hbm, fine_ref),
        geo=(geo_hbm, geo_ref), lag=(lag_hbm, lag_ref),
    )
    loads = {name: pltpu.make_async_copy(*refs, in_sem.at[i]) for i, (name, refs) in enumerate(copies.items())}
    for name in ("geo", "taps", "x", "tw", "fine"):
        loads[name].start()
    for load in lev_loads:
        load.start()
    loads["lag"].start()

    other = 1 - 2 * y_lo
    plane = [h for h in np.ndindex(4, 4, 2) if any(h)]
    plane.sort(key=lambda h: -(min(h[0], 4 - h[0]) + min(h[1], 4 - h[1])))
    plane = [tuple(map(int, h)) for h in plane]
    friends = [device(dx, dy, 0, dc) for dx, dy, dc in plane] + [device(0, e, d, 0) for d in (4, 3, 5, 2, 6, 1, 7) for e in (other, 0)]
    barrier = pltpu.get_barrier_semaphore()
    for friend in friends:
        pl.semaphore_signal(barrier, inc=1, device_id=friend, device_id_type=MESH)

    def remote(src, dst, send, recv, to):
        return pltpu.make_async_remote_copy(
            src_ref=src, dst_ref=dst, send_sem=send, recv_sem=recv, device_id=to, device_id_type=MESH
        )

    sibling = device(0, 0, 0, 1)
    loads["geo"].wait()
    dx, dy, dc = (geo_ref[pl.ds(i, 1), :] for i in range(3))
    kind = geo_ref[pl.ds(4, 1), :]
    xx, yy, cc = (x + dx) & 3, (y + dy) & 3, (core + dc) & 1
    source = 24 * (16 * (yy & 1) + 8 * cc + 4 * (yy >> 1) + xx) + geo_ref[pl.ds(3, 1), :]
    pick_ref[...] = (lax.broadcasted_iota(jnp.int32, (LEVEL, DEPTH), 0) == source).astype(F32).astype(BF16)
    white = whiten(x_ref, taps_ref[...], tw_ref, fine_ref, tap_ref, hi_ref, lo_ref, loads)
    blocks = len(HALF)
    mine = bbuf.at[0, blocks - 1]
    mine[...] = fold(jnp.concatenate(white, axis=1), 256)

    order = (1, 7, 2, 6, 3, 5, 4)
    slot_of = {d: n for n, d in enumerate(order)}
    for load in lev_loads:
        load.wait()
    picked = dot(lev_ref[...].reshape(8 * ROWS, LEVEL).astype(F32).astype(BF16), pick_ref[...])
    pl.semaphore_wait(barrier, len(friends))
    for n, (dx, dy) in enumerate(HALF[:-1]):
        remote(mine, bbuf.at[0, n], b_send, b_recv.at[int(n >= FAR)], device(4 - dx, 4 - dy, 0, 0)).start()
    for d in order:
        above = (mod(z + d, 8) > z).astype(jnp.int32)
        keep = jnp.broadcast_to(kind <= above, (ROWS, DEPTH))
        bsend[d - 1] = fold(jnp.where(keep, picked[ROWS * d : ROWS * d + ROWS], -1.0), 256)
    own = 24 * me + lax.broadcasted_iota(jnp.int32, (ROWS, DEPTH), 0)
    codes_ref[pl.ds(0, ROWS), :] = jnp.where((kind < 2) & (source > own), picked[:ROWS], -1.0)
    codes_ref[pl.ds(ROWS, ROWS), :] = jnp.where((kind < 1) & (source < own), picked[:ROWS], -1.0)
    for d in order:
        n = slot_of[8 - d]
        remote(bsend.at[d - 1], brecv.at[n], c_send, c_recv.at[n], device(0, 0, d, 0)).start()
        remote(mine, abuf.at[n], a_send, a_recv.at[n], device(0, 0, d, 0)).start()

    def set_rows(slot, rows, sign):
        tiles = [rows[:, 128 * t : 128 * t + 128] for t in range(3)]
        at = pl.ds(pl.multiple_of(ROWS * slot, 8), ROWS)
        for t, (one, two) in enumerate(zip(tiles, swap(tiles))):
            wa_ref[at, pl.ds(128 * t, 128)] = one
            wa_ref[at, pl.ds(384 + 128 * t, 128)] = two * sign

    def block_of(ref):
        return unfold(ref[...], 384, 256)

    bins = lax.broadcasted_iota(jnp.int32, (64, 128), 0).astype(F32).astype(BF16)

    def one_hots(out, slot, part):
        codes = codes_ref[pl.ds(pl.multiple_of(ROWS * slot, 8), ROWS), :]
        for a in range(12):
            row = codes[12 * part + a : 12 * part + a + 1]
            for t in range(4):
                lanes = pl.ds(128 * t, 128)
                code = jnp.broadcast_to(row[:, 128 * t : 128 * t + 128], (16, 128)).astype(BF16)
                for k in range(4):
                    out[pl.ds(64 * a + 16 * k, 16), lanes] = jnp.where(
                        code == bins[16 * k : 16 * k + 16], jnp.ones((), BF16), jnp.zeros((), BF16)
                    )

    def take(slot, part, ref):
        rows = pl.ds(pl.multiple_of(ROWS * slot, 8), ROWS)
        for t in range(3):
            lanes, more = pl.ds(128 * t, 128), pl.ds(384 + 128 * t, 128)
            w, v = wa_ref[rows, lanes], wa_ref[rows, more]
            xs, ys = x_acc[:, lanes], y_acc[:, lanes]
            for a in range(12):
                at = 12 * part + a
                piece = ref[pl.ds(64 * a, 64), lanes]
                xs = xs + w[at : at + 1] * piece
                ys = ys + v[at : at + 1] * piece
            x_acc[:, lanes] = xs
            y_acc[:, lanes] = ys

    one_hots(hot0, 0, 0)
    rows = block_of(mine)
    set_rows(0, rows, 1.0)
    set_rows(1, rows, -1.0)
    x_acc[...] = jnp.zeros_like(x_acc)
    y_acc[...] = jnp.zeros_like(y_acc)
    s1[...] = jnp.zeros_like(s1)
    loads["lag"].wait()
    lag_hi, lag_lo = halves(lag_ref[...])
    lhi_ref[...] = lag_hi
    llo_ref[...] = lag_lo
    bmat[pl.ds(2 * ROWS * blocks, DEPTH - 2 * ROWS * blocks), :] = jnp.zeros((DEPTH - 2 * ROWS * blocks, 384), BF16)
    groups = (pl.ds(FAR, blocks - FAR), pl.ds(0, FAR))
    near = bbuf.at[0, pl.ds(FAR, blocks - 1 - FAR)]
    far = bbuf.at[0, pl.ds(0, FAR)]

    def share(k):
        at = groups[k]
        return remote(bbuf.at[0, at], bbuf.at[1, at], s_send, s_recv.at[k], sibling)

    def assemble(k, first, last):
        for n in range(first, last, 2):
            two = [block_of(bbuf.at[k, m]) for m in (n, n + 1)]
            bmat[pl.ds(ROWS * (blocks * k + n), 2 * ROWS), :] = jnp.concatenate(two, axis=0).astype(BF16)

    remote(near, near, b_send, b_recv.at[1], sibling).wait_recv()
    share(0).start()
    assemble(0, FAR + 1, blocks)
    remote(far, far, b_send, b_recv.at[0], sibling).wait_recv()
    share(1).start()
    assemble(0, 0, FAR + 1)
    share(0).wait_recv()
    assemble(1, FAR + 1, blocks)
    share(1).wait_recv()
    assemble(1, 0, FAR + 1)

    def body(slot, carry):
        after = slot + 1

        @pl.when((slot > 0) & (slot < 8))
        def _():
            n = slot - 1
            remote(brecv.at[n], brecv.at[n], c_send, c_recv.at[n], sibling).wait_recv()
            codes_ref[pl.ds(pl.multiple_of(ROWS * after, 8), ROWS), :] = unfold(brecv[n], 512, 256)

        @pl.when(slot > 1)
        def _():
            n = slot - 2
            remote(abuf.at[n], abuf.at[n], a_send, a_recv.at[n], sibling).wait_recv()
            k = lax.div(slot, jnp.int32(2))
            d = k + mod(slot, 2) * (8 - 2 * k)
            below = (mod(z + d, 8) < z).astype(F32)
            set_rows(slot, block_of(abuf.at[n]), 2.0 * below - 1.0)

        s0[...] = dot(hot0[...], bmat[...])
        one_hots(hot1, slot, 1)
        take(jnp.maximum(slot - 1, 0), 1, s1)
        s1[...] = dot(hot1[...], bmat[...])
        one_hots(hot0, jnp.minimum(after, 8), 0)
        take(slot, 0, s0)
        return carry

    lax.fori_loop(0, 9, body, 0)
    take(8, 1, s1)

    xs = [x_acc[:, pl.ds(128 * t, 128)] for t in range(3)]
    ys = [y_acc[:, pl.ds(128 * t, 128)] for t in range(3)]
    sums = [xs[0] + xs[2], xs[1] + unpack(xs, 64), ys[0] - ys[2], ys[1] - unpack(ys, 64)]
    for t in range(4):
        for k in range(8):
            part[k, t] = sums[t][8 * k : 8 * k + 8]

    at = 4 * place + quad
    r1[at] = part[place, quad]
    for n, (dx, dy, dc) in enumerate(plane):
        to = device(dx, dy, 0, dc)
        remote(part.at[to[1], mod(to[0], 4)], r1.at[at], r1_send, r1_recv, to).start()
    remote(r1.at[pl.ds(0, 31)], r1.at[pl.ds(0, 31)], r1_send, r1_recv, sibling).wait_recv()

    def total(ref, n):
        values = [ref[i] for i in range(n)]
        while len(values) > 1:
            values = [a + b for a, b in zip(values[::2], values[1::2])]
        return values[0]

    r2[y_lo, z] = total(r1, 32)
    for d in (4, 3, 5, 2, 6, 1, 7, 0):
        for e in (other, 0) if d else (other,):
            remote(r2.at[y_lo, z], r2.at[y_lo, z], r2_send, r2_recv, device(0, e, d, 0)).start()
    most = r1.at[pl.ds(0, 15)]
    remote(most, most, r2_send, r2_recv, sibling).wait_recv()
    for k in range(2):
        r3[core, k] = total(r2.at[k], 8)
    remote(r3.at[core], r3.at[core], r3_send, r3_recv, sibling).start()
    remote(r3.at[core], r3.at[core], r3_send, r3_recv, sibling).wait_recv()
    hi, lo = halves(jnp.concatenate([r3[t % 2, t // 2] for t in range(4)], axis=1))
    both = jnp.concatenate([hi.astype(F32), lo.astype(F32)], axis=0).astype(BF16)
    out = dot(both, lhi_ref[...]) + dot(both, llo_ref[...])
    out_ref[...] = out[:8] + out[8:]
    for src, send, recv in (
        (bbuf.at[0, pl.ds(0, blocks - 1)], b_send, b_recv.at[0]), (bbuf.at[0], s_send, s_recv.at[0]), (abuf, a_send, a_recv.at[0]), (bsend, c_send, c_recv.at[0]),
        (r1.at[pl.ds(0, 31)], r1_send, r1_recv), (most, r2_send, r2_recv), (r3.at[0], r3_send, r3_recv),
    ):
        remote(src, src, send, recv, sibling).wait_send()


def solution(mesh):
    tables = make_tables()
    any_space = pl.BlockSpec(memory_space=pl.ANY)
    vmem = pl.BlockSpec(memory_space=pltpu.VMEM)
    dma = pltpu.SemaphoreType.DMA

    def step(traces, fir_taps, pair_bin):
        return pl.pallas_call(
            kernel,
            out_shape=jax.ShapeDtypeStruct((8, LAGS), F32),
            in_specs=[any_space, vmem, any_space] + [any_space] * len(tables),
            out_specs=vmem,
            scratch_shapes=[
                pltpu.VMEM((ROWS, SAMPLES), F32),
                *[pltpu.VMEM(t.shape, t.dtype) for t in tables],
                pltpu.VMEM((8, ROWS, LEVEL), jnp.int32),
                pltpu.VMEM((LEVEL, DEPTH), BF16),
                pltpu.VMEM((16 * ROWS, 512), BF16),
                pltpu.VMEM((16 * ROWS, 512), BF16),
                pltpu.VMEM((512, 512), BF16),
                pltpu.VMEM((512, 512), BF16),
                pltpu.VMEM((2, len(HALF), 16, 640), BF16),
                pltpu.VMEM((7, 16, 640), BF16),
                pltpu.VMEM((7, 16, 768), BF16),
                pltpu.VMEM((7, 16, 768), BF16),
                pltpu.VMEM((9 * ROWS, DEPTH), F32),
                pltpu.VMEM((9 * ROWS, 768), F32),
                pltpu.VMEM((12 * NBINS, DEPTH), BF16),
                pltpu.VMEM((12 * NBINS, DEPTH), BF16),
                pltpu.VMEM((DEPTH, 384), BF16),
                pltpu.VMEM((12 * NBINS, 384), F32),
                pltpu.VMEM((12 * NBINS, 384), F32),
                pltpu.VMEM((64, 384), F32),
                pltpu.VMEM((64, 384), F32),
                pltpu.VMEM((8, 4, 8, 128), F32),
                pltpu.VMEM((32, 8, 128), F32),
                pltpu.VMEM((2, 8, 8, 128), F32),
                pltpu.VMEM((2, 2, 8, 128), F32),
                dma((7,)),
                dma((8,)),
                dma(()),
                dma((2,)),
                dma(()),
                dma((2,)),
                dma(()),
                dma((7,)),
                dma(()),
                dma((7,)),
                dma(()),
                dma(()),
                dma(()),
                dma(()),
                dma(()),
                dma(()),
            ],
            compiler_params=pltpu.CompilerParams(
                collective_id=0, has_side_effects=True, vmem_limit_bytes=56 * 2**20
            ),
            name="stack",
        )(traces, fir_taps.reshape(1, TAPS), pair_bin, *[jnp.asarray(t) for t in tables])

    return jax.shard_map(
        step,
        mesh=mesh,
        in_specs=(P(("chan", "bin"), None), P(), P(("chan", "bin"), None)),
        out_specs=P("bin", None),
        check_vma=False,
    )
```

```python
import math

import jax
import jax.numpy as jnp
import numpy as np
from jax import lax
from jax.experimental import pallas as pl
from jax.experimental.pallas import tpu as pltpu
from jax.sharding import PartitionSpec as P

SAMPLES = 4096
TAPS = 64
BAND_LO = 64
NF = 192
MARGIN = 32
LAGS = 512
NBINS = 64
ROWS = 24
LEVEL = 768
MESH = pl.DeviceIdType.MESH
F32 = jnp.float32
BF16 = jnp.bfloat16


def lane_freqs():
    lane = np.arange(128)
    return np.concatenate([16 * (lane % 16) + 8 * j + lane // 16 for j in range(2)])


HALF = [(2, 2), (1, 2), (2, 3), (3, 1), (3, 3), (2, 0), (0, 2), (1, 0), (0, 1), (0, 0)]
FAR = 5
DEPTH = 512


def geometry():
    table = np.zeros((8, DEPTH), np.int32)
    table[3], table[4] = -4096, 2
    for far, dc, n in np.ndindex(2, 2, FAR):
        start = DEPTH // 2 * far + ROWS * (FAR * dc + n)
        at = slice(start, start + ROWS)
        h = HALF[n + FAR * (1 - far)]
        table[:3, at] = np.array((*h, dc))[:, None]
        table[3, at] = np.arange(ROWS)
        table[4, at] = not any(v % 2 for v in h)
    return table


def make_tables():
    e = lane_freqs()
    u = np.arange(256)
    ang = 2 * math.pi / SAMPLES * ((u[None, :] * np.arange(16)[:, None]) % SAMPLES)
    twiddle = np.concatenate([np.cos(ang), np.sin(ang)], 0).astype(np.float32)
    p = 2 + np.arange(128) % 16
    ang = 2 * math.pi / 256 * ((u[:, None] * p[None, :]) % 256)
    c, s = np.cos(ang), np.sin(ang)
    fine = np.concatenate([c, s], 1)
    ang = 2 * math.pi / SAMPLES * ((np.arange(TAPS)[:, None] * (32 + e)[None, :]) % SAMPLES)
    taps = np.concatenate([np.cos(ang), -np.sin(ang)], 1)
    f = e - MARGIN
    ok = (f >= 0) & (f < NF)
    phase = ((BAND_LO + np.where(ok, f, 0))[:, None] * (np.arange(LAGS) - LAGS // 2)[None, :]) % SAMPLES
    ang = 2 * math.pi / SAMPLES * phase
    lag = np.concatenate([np.cos(ang), -np.sin(ang)], 0) * (2.0 / SAMPLES) * np.concatenate([ok, ok])[:, None]
    return [t.astype(np.float32) for t in (twiddle, fine, taps, lag)] + [geometry()]


def dot(a, b, **kw):
    return jnp.dot(a, b, preferred_element_type=F32, **kw)


def halves(a):
    hi = a.astype(BF16)
    return hi, (a - hi.astype(F32)).astype(BF16)


def sixteen(x):
    root = math.sqrt(0.5)
    a = [x[k] + x[k + 8] for k in range(8)]
    b = [x[k] - x[k + 8] for k in range(8)]
    c = [a[k] + a[k + 4] for k in range(4)]
    d = [a[k] - a[k + 4] for k in range(4)]
    y = [None] * 9
    zero = jnp.zeros_like(x[0])
    even, odd = c[0] + c[2], c[1] + c[3]
    y[0] = (even + odd, zero)
    y[8] = (even - odd, zero)
    y[4] = (c[0] - c[2], c[3] - c[1])
    m, n = (d[1] - d[3]) * root, (d[1] + d[3]) * root
    y[2] = (d[0] + m, -(n + d[2]))
    y[6] = (d[0] - m, d[2] - n)
    for r in (1, 3, 5, 7):
        re, im = b[0], b[4] * (-1.0 if r % 4 == 1 else 1.0)
        for k in (1, 2, 3):
            re = re + (b[k] - b[8 - k]) * math.cos(math.pi * k * r / 8)
            im = im - (b[k] + b[8 - k]) * math.sin(math.pi * k * r / 8)
        y[r] = (re, im)
    return y


def freq_of(shape, axis):
    i = lax.broadcasted_iota(jnp.int32, shape, axis)
    return 16 * (i & 15) + 8 * (i >> 7) + ((i >> 4) & 7)


def whiten(x_ref, taps, tw_ref, fine_ref, tap_table, hi_ref, lo_ref, loads):
    padded = jnp.concatenate([taps, jnp.zeros((1, 64), F32)], axis=1)
    shifted = pltpu.roll(jnp.broadcast_to(padded, (128, 128)), 0, 1, stride=1, stride_axis=0)
    target = freq_of((256, 256), 1)
    apart = freq_of((256, 256), 0) - target
    win = jnp.where((apart >= -MARGIN) & (apart < MARGIN), 0.5 / MARGIN, 0.0).astype(BF16)
    loads["taps"].wait()
    gains = dot(shifted[:, :TAPS], tap_table[...], precision=lax.Precision.HIGHEST)
    loads["x"].wait()
    loads["tw"].wait()

    def body(i, carry):
        rows = pl.ds(pl.multiple_of(8 * i, 8), 8)
        for j in range(2):
            lanes = pl.ds(128 * j, 128)
            y = sixteen([x_ref[rows, pl.ds(256 * w + 128 * j, 128)] for w in range(16)])
            parts = []
            for r in range(16):
                re, im = y[min(r, 16 - r)]
                if r > 8:
                    im = -im
                if r:
                    c, s = tw_ref[pl.ds(r, 1), lanes], tw_ref[pl.ds(16 + r, 1), lanes]
                    re, im = re * c + im * s, im * c - re * s
                parts.append((re, im))
            for r in range(0, 16, 2):
                at = pl.ds(pl.multiple_of(128 * i + 8 * r, 16), 16)
                for k in range(2):
                    hi, lo = halves(jnp.concatenate([parts[r][k], parts[r + 1][k]], axis=0))
                    hi_ref[at, pl.ds(256 * k + 128 * j, 128)] = hi
                    lo_ref[at, pl.ds(256 * k + 128 * j, 128)] = lo
        return carry

    lax.fori_loop(0, 3, body, 0)
    loads["fine"].wait()
    both = fine_ref[...]
    c, s = halves(both[:, :128]), halves(both[:, 128:])
    fine = [jnp.concatenate([jnp.concatenate([c[k], -s[k]], 1), jnp.concatenate([s[k], c[k]], 1)], 0) for k in range(2)]
    left = jnp.concatenate([hi_ref[...], lo_ref[...], hi_ref[...]], axis=1)
    z = dot(left, jnp.concatenate([fine[0], fine[0], fine[1]], axis=0))
    lane = lax.broadcasted_iota(jnp.int32, (24, 128), 1)
    ext = []
    for part in range(2):
        for j in range(2):
            tile = jnp.zeros((24, 128), F32)
            for r in range(8):
                at = 8 * (8 * j + r)
                piece = jnp.concatenate([z[128 * i + at : 128 * i + at + 8, 128 * part : 128 * part + 128] for i in range(3)], 0)
                tile = jnp.where(lane // 16 == r, piece, tile)
            ext.append(tile)
    last = jnp.where(lane >= 64, x_ref[:, pl.ds(SAMPLES - 128, 128)], 0.0)
    cut = dot(last, gains, precision=lax.Precision.HIGHEST)
    h = [gains[0:1, 128 * k : 128 * k + 128] for k in range(4)]
    re = [h[j] * ext[j] - h[2 + j] * ext[2 + j] - cut[:, 128 * j : 128 * j + 128] for j in range(2)]
    im = [h[j] * ext[2 + j] + h[2 + j] * ext[j] - cut[:, 256 + 128 * j : 384 + 128 * j] for j in range(2)]
    power = jnp.concatenate([re[j] * re[j] + im[j] * im[j] for j in range(2)], axis=1)
    one = power.astype(BF16)
    rest = power - one.astype(F32)
    two = rest.astype(BF16)
    three = (rest - two.astype(F32)).astype(BF16)
    smooth = dot(one, win) + dot(two, win) + dot(three, win)
    scale = 1.0 / jnp.sqrt(smooth + 1e-06)
    r0, r1 = (re[j] * scale[:, 128 * j : 128 * j + 128] for j in range(2))
    i0, i1 = (im[j] * scale[:, 128 * j : 128 * j + 128] for j in range(2))
    slot = lane % 16
    band = (slot >= 2) & (slot < 14)

    def pack(a, b, c, d):
        return [
            jnp.where(band, t, pltpu.roll(d, s, 1)) for t, s in ((a, 12), (b, 8), (c, 4))
        ]

    return pack(r0, r1, i0, i1)


def swap(tiles):
    a, b, c = tiles
    slot = lax.broadcasted_iota(jnp.int32, (ROWS, 128), 1) % 16
    band = (slot >= 2) & (slot < 14)
    full = (c, unpack(tiles, ROWS), a)
    return [jnp.where(band, t, pltpu.roll(b, s, 1)) for t, s in zip(full, (12, 8, 4))]


def unpack(tiles, rows):
    slot = lax.broadcasted_iota(jnp.int32, (rows, 128), 1) % 16
    a, b, c = (pltpu.roll(t, s, 1) for t, s in zip(tiles, (116, 120, 124)))
    return jnp.where(slot < 6, a, jnp.where(slot < 10, b, c))


def mod(a, n):
    return lax.rem(a, jnp.int32(n))


def fold(rows, width):
    parts = [rows[16:, i : i + width] for i in range(0, rows.shape[1], width)]
    if parts[1].shape[1] < width:
        parts[1] = jnp.concatenate([parts[1], jnp.zeros((8, width - parts[1].shape[1]), F32)], axis=1)
    return jnp.concatenate([rows[:16], jnp.concatenate(parts, axis=0)], axis=1).astype(BF16)


def unfold(block, cols, width):
    wide = block.astype(F32)
    tail = [wide[:8, cols:], wide[8:, cols : 2 * cols - width]]
    return jnp.concatenate([wide[:, :cols], jnp.concatenate(tail, axis=1)], axis=0)


def kernel(
    x_hbm, taps_ref, bins_hbm, tw_hbm, fine_hbm, tap_hbm, lag_hbm, geo_hbm,
    out_ref,
    x_ref, tw_ref, fine_ref, tap_ref, lag_ref, geo_ref, lev_ref, pick_ref, hi_ref, lo_ref, lhi_ref, llo_ref,
    bbuf, abuf, bsend, brecv, codes_ref, wa_ref, hot_own, hot0, hot1, bmat, s0, s1, x_acc, y_acc, part, r1, r2, r3,
    in_sem, lev_sem, b_send, b_recv, s_send, s_recv, a_send, a_recv, c_send, c_recv,
    r1_send, r1_recv, r2_send, r2_recv, r3_send, r3_recv,
):
    chan, place = lax.axis_index("chan"), lax.axis_index("bin")
    z, quad = lax.div(chan, jnp.int32(4)), mod(chan, 4)
    y_lo, core = lax.div(quad, jnp.int32(2)), mod(quad, 2)
    y_hi, x = lax.div(place, jnp.int32(4)), mod(place, 4)
    y = 2 * y_hi + y_lo
    me = 16 * y_lo + 8 * core + place

    def device(dx, dy, dz, dc):
        xx, yy, zz, cc = mod(x + dx, 4), mod(y + dy, 4), mod(z + dz, 8), mod(core + dc, 2)
        return (4 * zz + 2 * mod(yy, 2) + cc, 4 * lax.div(yy, jnp.int32(2)) + xx)

    lev_loads = [
        pltpu.make_async_copy(
            bins_hbm.at[:, pl.ds(pl.multiple_of(mod(z + d, 8) * LEVEL, 128), LEVEL)], lev_ref.at[d], lev_sem.at[d]
        )
        for d in range(8)
    ]
    copies = dict(
        taps=(tap_hbm, tap_ref), x=(x_hbm, x_ref), tw=(tw_hbm, tw_ref), fine=(fine_hbm, fine_ref),
        geo=(geo_hbm, geo_ref), lag=(lag_hbm, lag_ref),
    )
    loads = {name: pltpu.make_async_copy(*refs, in_sem.at[i]) for i, (name, refs) in enumerate(copies.items())}
    for name in ("x", "tw", "taps", "fine", "geo"):
        loads[name].start()
    for load in lev_loads:
        load.start()
    loads["lag"].start()

    other = 1 - 2 * y_lo
    plane = [h for h in np.ndindex(4, 4, 2) if any(h)]
    plane.sort(key=lambda h: -(min(h[0], 4 - h[0]) + min(h[1], 4 - h[1])))
    plane = [tuple(map(int, h)) for h in plane]
    friends = [device(0, e, d, 0) for d in (4, 3, 5) for e in (other, 0)]
    friends += [device(dx, dy, 0, dc) for dx, dy, dc in plane]
    friends += [device(0, e, d, 0) for d in (2, 6, 1, 7) for e in (other, 0)]
    barrier = pltpu.get_barrier_semaphore()
    for friend in friends:
        pl.semaphore_signal(barrier, inc=1, device_id=friend, device_id_type=MESH)

    def remote(src, dst, send, recv, to):
        return pltpu.make_async_remote_copy(
            src_ref=src, dst_ref=dst, send_sem=send, recv_sem=recv, device_id=to, device_id_type=MESH
        )

    sibling = device(0, 0, 0, 1)
    white = whiten(x_ref, taps_ref[...], tw_ref, fine_ref, tap_ref, hi_ref, lo_ref, loads)
    blocks = len(HALF)
    mine = bbuf.at[0, blocks - 1]
    mine[...] = fold(jnp.concatenate(white, axis=1), 256)

    pl.semaphore_wait(barrier, len(friends))
    for n, (dx, dy) in enumerate(HALF[:-1]):
        remote(mine, bbuf.at[0, n], b_send, b_recv.at[int(n >= FAR)], device(4 - dx, 4 - dy, 0, 0)).start()

    loads["geo"].wait()
    dx, dy, dc = (geo_ref[pl.ds(i, 1), :] for i in range(3))
    kind = geo_ref[pl.ds(4, 1), :]
    xx, yy, cc = (x + dx) & 3, (y + dy) & 3, (core + dc) & 1
    source = 24 * (16 * (yy & 1) + 8 * cc + 4 * (yy >> 1) + xx) + geo_ref[pl.ds(3, 1), :]
    pick_ref[...] = (lax.broadcasted_iota(jnp.int32, (LEVEL, DEPTH), 0) == source).astype(F32).astype(BF16)
    order = (1, 7, 2, 6, 3, 5, 4)
    slot_of = {d: n for n, d in enumerate(order)}
    for load in lev_loads:
        load.wait()
    picked = dot(lev_ref[...].reshape(8 * ROWS, LEVEL).astype(F32).astype(BF16), pick_ref[...])
    for d in order:
        above = (mod(z + d, 8) > z).astype(jnp.int32)
        keep = jnp.broadcast_to(kind <= above, (ROWS, DEPTH))
        bsend[d - 1] = fold(jnp.where(keep, picked[ROWS * d : ROWS * d + ROWS], -1.0), 256)
    own = 24 * me + lax.broadcasted_iota(jnp.int32, (ROWS, DEPTH), 0)
    codes_ref[pl.ds(0, ROWS), :] = jnp.where((kind < 2) & (source > own), picked[:ROWS], -1.0)
    codes_ref[pl.ds(ROWS, ROWS), :] = jnp.where((kind < 1) & (source < own), picked[:ROWS], -1.0)
    for d in order:
        n = slot_of[8 - d]
        remote(bsend.at[d - 1], brecv.at[n], c_send, c_recv.at[n], device(0, 0, d, 0)).start()
        remote(mine, abuf.at[n], a_send, a_recv.at[n], device(0, 0, d, 0)).start()

    def set_rows(slot, rows, sign):
        tiles = [rows[:, 128 * t : 128 * t + 128] for t in range(3)]
        at = pl.ds(pl.multiple_of(ROWS * slot, 8), ROWS)
        for t, (one, two) in enumerate(zip(tiles, swap(tiles))):
            wa_ref[at, pl.ds(128 * t, 128)] = one
            wa_ref[at, pl.ds(384 + 128 * t, 128)] = two * sign

    def block_of(ref):
        return unfold(ref[...], 384, 256)

    bins = lax.broadcasted_iota(jnp.int32, (64, 128), 0).astype(F32).astype(BF16)

    def one_hots(out, slot, part):
        codes = codes_ref[pl.ds(pl.multiple_of(ROWS * slot, 8), ROWS), :]
        for a in range(12):
            row = codes[12 * part + a : 12 * part + a + 1]
            for t in range(4):
                lanes = pl.ds(128 * t, 128)
                code = jnp.broadcast_to(row[:, 128 * t : 128 * t + 128], (16, 128)).astype(BF16)
                for k in range(4):
                    out[pl.ds(64 * a + 16 * k, 16), lanes] = jnp.where(
                        code == bins[16 * k : 16 * k + 16], jnp.ones((), BF16), jnp.zeros((), BF16)
                    )

    def take(slot, part, ref):
        rows = pl.ds(pl.multiple_of(ROWS * slot, 8), ROWS)
        for t in range(3):
            lanes, more = pl.ds(128 * t, 128), pl.ds(384 + 128 * t, 128)
            w, v = wa_ref[rows, lanes], wa_ref[rows, more]
            xs, ys = x_acc[:, lanes], y_acc[:, lanes]
            for a in range(12):
                at = 12 * part + a
                piece = ref[pl.ds(64 * a, 64), lanes]
                xs = xs + w[at : at + 1] * piece
                ys = ys + v[at : at + 1] * piece
            x_acc[:, lanes] = xs
            y_acc[:, lanes] = ys

    def start(slot, carry):
        for part in range(2):
            at = pl.multiple_of(ROWS * NBINS * slot + 12 * NBINS * part, 16)
            one_hots(hot_own.at[pl.ds(at, 12 * NBINS)], slot, part)
        return carry

    lax.fori_loop(0, 2, start, 0)
    rows = block_of(mine)
    set_rows(0, rows, 1.0)
    set_rows(1, rows, -1.0)
    x_acc[...] = jnp.zeros_like(x_acc)
    y_acc[...] = jnp.zeros_like(y_acc)
    s1[...] = jnp.zeros_like(s1)
    loads["lag"].wait()
    lag_hi, lag_lo = halves(lag_ref[...])
    lhi_ref[...] = lag_hi
    llo_ref[...] = lag_lo
    for far in range(2):
        bmat[pl.ds(DEPTH // 2 * far + 240, 16), :] = jnp.zeros((16, 384), BF16)

    groups = (pl.ds(FAR, blocks - FAR), pl.ds(0, FAR))
    near = bbuf.at[0, pl.ds(FAR, blocks - 1 - FAR)]
    far = bbuf.at[0, pl.ds(0, FAR)]

    def share(k):
        at = groups[k]
        return remote(bbuf.at[0, at], bbuf.at[1, at], s_send, s_recv.at[k], sibling)

    def assemble(far):
        for i in range(FAR):
            two = [block_of(bbuf.at[m // FAR, m % FAR + FAR * (1 - far)]) for m in (2 * i, 2 * i + 1)]
            bmat[pl.ds(DEPTH // 2 * far + 2 * ROWS * i, 2 * ROWS), :] = jnp.concatenate(two, axis=0).astype(BF16)

    remote(near, near, b_send, b_recv.at[1], sibling).wait_recv()
    share(0).start()
    share(0).wait_recv()
    assemble(0)
    remote(far, far, b_send, b_recv.at[0], sibling).wait_recv()
    share(1).start()

    def own_body(step, carry):
        far, slot = lax.div(step, jnp.int32(2)), mod(step, 2)

        @pl.when(step == 2)
        def _():
            share(1).wait_recv()
            assemble(1)

        @pl.when(step == 3)
        def _():
            wait_codes(0)
            put_codes(0)

        half = pl.ds(pl.multiple_of(DEPTH // 2 * far, 256), DEPTH // 2)
        at = pl.multiple_of(ROWS * NBINS * slot, 16)
        s0[...] = dot(hot_own[pl.ds(at, 12 * NBINS), half], bmat[half, :])
        take(1 - slot, 1, s1)
        s1[...] = dot(hot_own[pl.ds(at + 12 * NBINS, 12 * NBINS), half], bmat[half, :])
        one_hots(hot0, 2, 0)
        take(slot, 0, s0)
        return carry

    def wait_codes(n):
        remote(brecv.at[n], brecv.at[n], c_send, c_recv.at[n], sibling).wait_recv()

    def put_codes(n):
        codes_ref[pl.ds(pl.multiple_of(ROWS * (n + 2), 8), ROWS), :] = unfold(brecv[n], 512, 256)

    lax.fori_loop(0, 4, own_body, 0)

    def body(slot, carry):
        @pl.when(slot < 8)
        def _():
            wait_codes(slot - 1)

        n, m = slot - 2, jnp.minimum(slot - 1, 6)
        remote(abuf.at[n], abuf.at[n], a_send, a_recv.at[n], sibling).wait_recv()
        s0[...] = dot(hot0[...], bmat[...])
        one_hots(hot1, slot, 1)
        take(slot - 1, 1, s1)
        put_codes(m)
        k = lax.div(slot, jnp.int32(2))
        d = k + mod(slot, 2) * (8 - 2 * k)
        below = (mod(z + d, 8) < z).astype(F32)
        set_rows(slot, block_of(abuf.at[n]), 2.0 * below - 1.0)
        s1[...] = dot(hot1[...], bmat[...])
        one_hots(hot0, m + 2, 0)
        take(slot, 0, s0)
        return carry

    lax.fori_loop(2, 9, body, 0)
    take(8, 1, s1)

    xs = [x_acc[:, pl.ds(128 * t, 128)] for t in range(3)]
    ys = [y_acc[:, pl.ds(128 * t, 128)] for t in range(3)]
    sums = [xs[0] + xs[2], xs[1] + unpack(xs, 64), ys[0] - ys[2], ys[1] - unpack(ys, 64)]
    for t in range(4):
        for k in range(8):
            part[k, t] = sums[t][8 * k : 8 * k + 8]

    at = 4 * place + quad
    r1[at] = part[place, quad]
    for n, (dx, dy, dc) in enumerate(plane):
        to = device(dx, dy, 0, dc)
        remote(part.at[to[1], mod(to[0], 4)], r1.at[at], r1_send, r1_recv, to).start()
    remote(r1.at[pl.ds(0, 31)], r1.at[pl.ds(0, 31)], r1_send, r1_recv, sibling).wait_recv()

    def total(ref, n):
        values = [ref[i] for i in range(n)]
        while len(values) > 1:
            values = [a + b for a, b in zip(values[::2], values[1::2])]
        return values[0]

    r2[y_lo, z] = total(r1, 32)
    for d in (4, 3, 5, 2, 6, 1, 7, 0):
        for e in (other, 0) if d else (other,):
            remote(r2.at[y_lo, z], r2.at[y_lo, z], r2_send, r2_recv, device(0, e, d, 0)).start()
    most = r1.at[pl.ds(0, 15)]
    remote(most, most, r2_send, r2_recv, sibling).wait_recv()
    for k in range(2):
        r3[core, k] = total(r2.at[k], 8)
    remote(r3.at[core], r3.at[core], r3_send, r3_recv, sibling).start()
    remote(r3.at[core], r3.at[core], r3_send, r3_recv, sibling).wait_recv()
    hi, lo = halves(jnp.concatenate([r3[t % 2, t // 2] for t in range(4)], axis=1))
    both = jnp.concatenate([hi.astype(F32), lo.astype(F32)], axis=0).astype(BF16)
    out = dot(both, lhi_ref[...]) + dot(both, llo_ref[...])
    out_ref[...] = out[:8] + out[8:]
    for src, send, recv in (
        (bbuf.at[0, pl.ds(0, blocks - 1)], b_send, b_recv.at[0]), (bbuf.at[0], s_send, s_recv.at[0]), (abuf, a_send, a_recv.at[0]), (bsend, c_send, c_recv.at[0]),
        (r1.at[pl.ds(0, 31)], r1_send, r1_recv), (most, r2_send, r2_recv), (r3.at[0], r3_send, r3_recv),
    ):
        remote(src, src, send, recv, sibling).wait_send()


def solution(mesh):
    tables = make_tables()
    any_space = pl.BlockSpec(memory_space=pl.ANY)
    vmem = pl.BlockSpec(memory_space=pltpu.VMEM)
    dma = pltpu.SemaphoreType.DMA

    def step(traces, fir_taps, pair_bin):
        return pl.pallas_call(
            kernel,
            out_shape=jax.ShapeDtypeStruct((8, LAGS), F32),
            in_specs=[any_space, vmem, any_space] + [any_space] * len(tables),
            out_specs=vmem,
            scratch_shapes=[
                pltpu.VMEM((ROWS, SAMPLES), F32),
                *[pltpu.VMEM(t.shape, t.dtype) for t in tables],
                pltpu.VMEM((8, ROWS, LEVEL), jnp.int32),
                pltpu.VMEM((LEVEL, DEPTH), BF16),
                pltpu.VMEM((16 * ROWS, 512), BF16),
                pltpu.VMEM((16 * ROWS, 512), BF16),
                pltpu.VMEM((512, 512), BF16),
                pltpu.VMEM((512, 512), BF16),
                pltpu.VMEM((2, len(HALF), 16, 640), BF16),
                pltpu.VMEM((7, 16, 640), BF16),
                pltpu.VMEM((7, 16, 768), BF16),
                pltpu.VMEM((7, 16, 768), BF16),
                pltpu.VMEM((9 * ROWS, DEPTH), F32),
                pltpu.VMEM((9 * ROWS, 768), F32),
                pltpu.VMEM((2 * ROWS * NBINS, DEPTH), BF16),
                pltpu.VMEM((12 * NBINS, DEPTH), BF16),
                pltpu.VMEM((12 * NBINS, DEPTH), BF16),
                pltpu.VMEM((DEPTH, 384), BF16),
                pltpu.VMEM((12 * NBINS, 384), F32),
                pltpu.VMEM((12 * NBINS, 384), F32),
                pltpu.VMEM((64, 384), F32),
                pltpu.VMEM((64, 384), F32),
                pltpu.VMEM((8, 4, 8, 128), F32),
                pltpu.VMEM((32, 8, 128), F32),
                pltpu.VMEM((2, 8, 8, 128), F32),
                pltpu.VMEM((2, 2, 8, 128), F32),
                dma((7,)),
                dma((8,)),
                dma(()),
                dma((2,)),
                dma(()),
                dma((2,)),
                dma(()),
                dma((7,)),
                dma(()),
                dma((7,)),
                dma(()),
                dma(()),
                dma(()),
                dma(()),
                dma(()),
                dma(()),
            ],
            compiler_params=pltpu.CompilerParams(
                collective_id=0, has_side_effects=True, vmem_limit_bytes=56 * 2**20
            ),
            name="stack",
        )(traces, fir_taps.reshape(1, TAPS), pair_bin, *[jnp.asarray(t) for t in tables])

    return jax.shard_map(
        step,
        mesh=mesh,
        in_specs=(P(("chan", "bin"), None), P(), P(("chan", "bin"), None)),
        out_specs=P("bin", None),
        check_vma=False,
    )
```

```python
import math

import jax
import jax.numpy as jnp
import numpy as np
from jax import lax
from jax.experimental import pallas as pl
from jax.experimental.pallas import tpu as pltpu
from jax.sharding import PartitionSpec as P

SAMPLES = 4096
TAPS = 64
BAND_LO = 64
NF = 192
MARGIN = 32
LAGS = 512
NBINS = 64
ROWS = 24
LEVEL = 768
MESH = pl.DeviceIdType.MESH
F32 = jnp.float32
BF16 = jnp.bfloat16


def lane_freqs():
    lane = np.arange(128)
    return np.concatenate([16 * (lane % 16) + 8 * j + lane // 16 for j in range(2)])


HALF = [(2, 2), (1, 2), (2, 3), (3, 1), (3, 3), (2, 0), (0, 2), (1, 0), (0, 1), (0, 0)]
FAR = 5
DEPTH = 512


def geometry():
    table = np.zeros((8, DEPTH), np.int32)
    table[3], table[4] = -4096, 2
    for far, dc, n in np.ndindex(2, 2, FAR):
        start = DEPTH // 2 * far + ROWS * (FAR * dc + n)
        at = slice(start, start + ROWS)
        h = HALF[n + FAR * (1 - far)]
        table[:3, at] = np.array((*h, dc))[:, None]
        table[3, at] = np.arange(ROWS)
        table[4, at] = not any(v % 2 for v in h)
    return table


def make_tables():
    e = lane_freqs()
    u = np.arange(256)
    ang = 2 * math.pi / SAMPLES * ((u[None, :] * np.arange(16)[:, None]) % SAMPLES)
    twiddle = np.concatenate([np.cos(ang), np.sin(ang)], 0).astype(np.float32)
    p = 2 + np.arange(128) % 16
    ang = 2 * math.pi / 256 * ((u[:, None] * p[None, :]) % 256)
    c, s = np.cos(ang), np.sin(ang)
    fine = np.concatenate([c, s], 1)
    ang = 2 * math.pi / SAMPLES * ((np.arange(TAPS)[:, None] * (32 + e)[None, :]) % SAMPLES)
    taps = np.concatenate([np.cos(ang), -np.sin(ang)], 1)
    f = e - MARGIN
    ok = (f >= 0) & (f < NF)
    phase = ((BAND_LO + np.where(ok, f, 0))[:, None] * (np.arange(LAGS) - LAGS // 2)[None, :]) % SAMPLES
    ang = 2 * math.pi / SAMPLES * phase
    lag = np.concatenate([np.cos(ang), -np.sin(ang)], 0) * (2.0 / SAMPLES) * np.concatenate([ok, ok])[:, None]
    return [t.astype(np.float32) for t in (twiddle, fine, taps, lag)] + [geometry()]


def dot(a, b, **kw):
    return jnp.dot(a, b, preferred_element_type=F32, **kw)


def halves(a):
    hi = a.astype(BF16)
    return hi, (a - hi.astype(F32)).astype(BF16)


def sixteen(x):
    root = math.sqrt(0.5)
    a = [x[k] + x[k + 8] for k in range(8)]
    b = [x[k] - x[k + 8] for k in range(8)]
    c = [a[k] + a[k + 4] for k in range(4)]
    d = [a[k] - a[k + 4] for k in range(4)]
    y = [None] * 9
    zero = jnp.zeros_like(x[0])
    even, odd = c[0] + c[2], c[1] + c[3]
    y[0] = (even + odd, zero)
    y[8] = (even - odd, zero)
    y[4] = (c[0] - c[2], c[3] - c[1])
    m, n = (d[1] - d[3]) * root, (d[1] + d[3]) * root
    y[2] = (d[0] + m, -(n + d[2]))
    y[6] = (d[0] - m, d[2] - n)
    for r in (1, 3, 5, 7):
        re, im = b[0], b[4] * (-1.0 if r % 4 == 1 else 1.0)
        for k in (1, 2, 3):
            re = re + (b[k] - b[8 - k]) * math.cos(math.pi * k * r / 8)
            im = im - (b[k] + b[8 - k]) * math.sin(math.pi * k * r / 8)
        y[r] = (re, im)
    return y


def freq_of(shape, axis):
    i = lax.broadcasted_iota(jnp.int32, shape, axis)
    return 16 * (i & 15) + 8 * (i >> 7) + ((i >> 4) & 7)


def whiten(x_ref, taps, tw_ref, fine_ref, tap_table, hi_ref, lo_ref, loads):
    padded = jnp.concatenate([taps, jnp.zeros((1, 64), F32)], axis=1)
    shifted = pltpu.roll(jnp.broadcast_to(padded, (128, 128)), 0, 1, stride=1, stride_axis=0)
    target = freq_of((256, 256), 1)
    apart = freq_of((256, 256), 0) - target
    win = jnp.where((apart >= -MARGIN) & (apart < MARGIN), 0.5 / MARGIN, 0.0).astype(BF16)
    loads["taps"].wait()
    gains = dot(shifted[:, :TAPS], tap_table[...], precision=lax.Precision.HIGHEST)
    tail_hi, tail_lo = halves(gains[TAPS:])
    right_cut = jnp.concatenate([tail_hi, tail_hi, tail_lo, jnp.zeros_like(tail_hi)], axis=0)
    loads["x"].wait()
    last = x_ref[:, pl.ds(SAMPLES - 128, 128)]
    last_hi = last.astype(BF16).astype(F32)
    first_lanes = lax.broadcasted_iota(jnp.int32, (24, 128), 1) < 64
    moved = pltpu.roll(last_hi, 64, 1)
    pieces = [jnp.where(first_lanes, moved, last - last_hi), jnp.where(first_lanes, moved, 0.0)]
    left_cut = jnp.concatenate(pieces, axis=1).astype(BF16)
    loads["tw"].wait()

    def body(i, carry):
        rows = pl.ds(pl.multiple_of(8 * i, 8), 8)
        for j in range(2):
            lanes = pl.ds(128 * j, 128)
            y = sixteen([x_ref[rows, pl.ds(256 * w + 128 * j, 128)] for w in range(16)])
            parts = []
            for r in range(16):
                re, im = y[min(r, 16 - r)]
                if r > 8:
                    im = -im
                if r:
                    c, s = tw_ref[pl.ds(r, 1), lanes], tw_ref[pl.ds(16 + r, 1), lanes]
                    re, im = re * c + im * s, im * c - re * s
                parts.append((re, im))
            for r in range(0, 16, 2):
                at = pl.ds(pl.multiple_of(128 * i + 8 * r, 16), 16)
                for k in range(2):
                    hi, lo = halves(jnp.concatenate([parts[r][k], parts[r + 1][k]], axis=0))
                    hi_ref[at, pl.ds(256 * k + 128 * j, 128)] = hi
                    lo_ref[at, pl.ds(256 * k + 128 * j, 128)] = lo
        return carry

    lax.fori_loop(0, 3, body, 0)
    loads["fine"].wait()
    both = fine_ref[...]
    c, s = halves(both[:, :128]), halves(both[:, 128:])
    fine = [jnp.concatenate([jnp.concatenate([c[k], -s[k]], 1), jnp.concatenate([s[k], c[k]], 1)], 0) for k in range(2)]
    left = jnp.concatenate([hi_ref[...], lo_ref[...], hi_ref[...]], axis=1)
    z = dot(left, jnp.concatenate([fine[0], fine[0], fine[1]], axis=0))
    lane = lax.broadcasted_iota(jnp.int32, (24, 128), 1)
    ext = []
    for part in range(2):
        for j in range(2):
            tile = jnp.zeros((24, 128), F32)
            for r in range(8):
                at = 8 * (8 * j + r)
                piece = jnp.concatenate([z[128 * i + at : 128 * i + at + 8, 128 * part : 128 * part + 128] for i in range(3)], 0)
                tile = jnp.where(lane // 16 == r, piece, tile)
            ext.append(tile)
    cut = dot(left_cut, right_cut)
    h = [gains[0:1, 128 * k : 128 * k + 128] for k in range(4)]
    re = [h[j] * ext[j] - h[2 + j] * ext[2 + j] - cut[:, 128 * j : 128 * j + 128] for j in range(2)]
    im = [h[j] * ext[2 + j] + h[2 + j] * ext[j] - cut[:, 256 + 128 * j : 384 + 128 * j] for j in range(2)]
    power = jnp.concatenate([re[j] * re[j] + im[j] * im[j] for j in range(2)], axis=1)
    one = power.astype(BF16).astype(F32)
    two = (power - one).astype(BF16).astype(F32)
    sums = dot(jnp.concatenate([one, two, power - one - two], axis=0).astype(BF16), win)
    smooth = sums[:24] + sums[24:48] + sums[48:]
    scale = 1.0 / jnp.sqrt(smooth + 1e-06)
    r0, r1 = (re[j] * scale[:, 128 * j : 128 * j + 128] for j in range(2))
    i0, i1 = (im[j] * scale[:, 128 * j : 128 * j + 128] for j in range(2))
    slot = lane % 16
    band = (slot >= 2) & (slot < 14)

    def pack(a, b, c, d):
        return [
            jnp.where(band, t, pltpu.roll(d, s, 1)) for t, s in ((a, 12), (b, 8), (c, 4))
        ]

    return pack(r0, r1, i0, i1)


def swap(tiles):
    a, b, c = tiles
    slot = lax.broadcasted_iota(jnp.int32, (ROWS, 128), 1) % 16
    band = (slot >= 2) & (slot < 14)
    full = (c, unpack(tiles, ROWS), a)
    return [jnp.where(band, t, pltpu.roll(b, s, 1)) for t, s in zip(full, (12, 8, 4))]


def unpack(tiles, rows):
    slot = lax.broadcasted_iota(jnp.int32, (rows, 128), 1) % 16
    a, b, c = (pltpu.roll(t, s, 1) for t, s in zip(tiles, (116, 120, 124)))
    return jnp.where(slot < 6, a, jnp.where(slot < 10, b, c))


def mod(a, n):
    return lax.rem(a, jnp.int32(n))


def fold(rows, width):
    parts = [rows[16:, i : i + width] for i in range(0, rows.shape[1], width)]
    if parts[1].shape[1] < width:
        parts[1] = jnp.concatenate([parts[1], jnp.zeros((8, width - parts[1].shape[1]), F32)], axis=1)
    return jnp.concatenate([rows[:16], jnp.concatenate(parts, axis=0)], axis=1).astype(BF16)


def unfold(block, cols, width):
    wide = block.astype(F32)
    tail = [wide[:8, cols:], wide[8:, cols : 2 * cols - width]]
    return jnp.concatenate([wide[:, :cols], jnp.concatenate(tail, axis=1)], axis=0)


def kernel(
    x_hbm, taps_ref, bins_hbm, tw_hbm, fine_hbm, tap_hbm, lag_hbm, geo_hbm,
    out_ref,
    x_ref, tw_ref, fine_ref, tap_ref, lag_ref, geo_ref, lev_ref, pick_ref, hi_ref, lo_ref, lhi_ref, llo_ref,
    bbuf, abuf, bsend, brecv, codes_ref, wa_ref, hot_own, hot0, hot1, bmat, s0, s1, x_acc, y_acc, part, r1, r2, r3,
    in_sem, lev_sem, b_send, b_recv, s_send, s_recv, a_send, a_recv, c_send, c_recv,
    r1_send, r1_recv, r2_send, r2_recv, r3_send, r3_recv,
):
    chan, place = lax.axis_index("chan"), lax.axis_index("bin")
    z, quad = lax.div(chan, jnp.int32(4)), mod(chan, 4)
    y_lo, core = lax.div(quad, jnp.int32(2)), mod(quad, 2)
    y_hi, x = lax.div(place, jnp.int32(4)), mod(place, 4)
    y = 2 * y_hi + y_lo
    me = 16 * y_lo + 8 * core + place

    def device(dx, dy, dz, dc):
        xx, yy, zz, cc = mod(x + dx, 4), mod(y + dy, 4), mod(z + dz, 8), mod(core + dc, 2)
        return (4 * zz + 2 * mod(yy, 2) + cc, 4 * lax.div(yy, jnp.int32(2)) + xx)

    lev_loads = [
        pltpu.make_async_copy(
            bins_hbm.at[:, pl.ds(pl.multiple_of(mod(z + d, 8) * LEVEL, 128), LEVEL)], lev_ref.at[d], lev_sem.at[d]
        )
        for d in range(8)
    ]
    copies = dict(
        taps=(tap_hbm, tap_ref), x=(x_hbm, x_ref), tw=(tw_hbm, tw_ref), fine=(fine_hbm, fine_ref),
        geo=(geo_hbm, geo_ref), lag=(lag_hbm, lag_ref),
    )
    loads = {name: pltpu.make_async_copy(*refs, in_sem.at[i]) for i, (name, refs) in enumerate(copies.items())}
    for name in ("x", "tw", "taps", "fine", "geo"):
        loads[name].start()
    for load in lev_loads:
        load.start()
    loads["lag"].start()

    other = 1 - 2 * y_lo
    plane = [h for h in np.ndindex(4, 4, 2) if any(h)]
    plane.sort(key=lambda h: -(min(h[0], 4 - h[0]) + min(h[1], 4 - h[1])))
    plane = [tuple(map(int, h)) for h in plane]
    friends = [device(0, e, d, 0) for d in (4, 3, 5) for e in (other, 0)]
    friends += [device(dx, dy, 0, dc) for dx, dy, dc in plane]
    friends += [device(0, e, d, 0) for d in (2, 6, 1, 7) for e in (other, 0)]
    barrier = pltpu.get_barrier_semaphore()
    for friend in friends:
        pl.semaphore_signal(barrier, inc=1, device_id=friend, device_id_type=MESH)

    def remote(src, dst, send, recv, to):
        return pltpu.make_async_remote_copy(
            src_ref=src, dst_ref=dst, send_sem=send, recv_sem=recv, device_id=to, device_id_type=MESH
        )

    sibling = device(0, 0, 0, 1)
    white = whiten(x_ref, taps_ref[...], tw_ref, fine_ref, tap_ref, hi_ref, lo_ref, loads)
    blocks = len(HALF)
    mine = bbuf.at[0, blocks - 1]
    mine[...] = fold(jnp.concatenate(white, axis=1), 256)

    pl.semaphore_wait(barrier, len(friends))
    order = (1, 7, 2, 6, 3, 5, 4)
    slot_of = {d: n for n, d in enumerate(order)}
    for n, (dx, dy) in enumerate(HALF[:-1]):
        remote(mine, bbuf.at[0, n], b_send, b_recv.at[int(n >= FAR)], device(4 - dx, 4 - dy, 0, 0)).start()

    for d in order:
        n = slot_of[8 - d]
        remote(mine, abuf.at[n], a_send, a_recv.at[n], device(0, 0, d, 0)).start()

    loads["geo"].wait()
    dx, dy, dc = (geo_ref[pl.ds(i, 1), :] for i in range(3))
    kind = geo_ref[pl.ds(4, 1), :]
    xx, yy, cc = (x + dx) & 3, (y + dy) & 3, (core + dc) & 1
    source = 24 * (16 * (yy & 1) + 8 * cc + 4 * (yy >> 1) + xx) + geo_ref[pl.ds(3, 1), :]
    pick_ref[...] = (lax.broadcasted_iota(jnp.int32, (LEVEL, DEPTH), 0) == source).astype(F32).astype(BF16)
    for load in lev_loads:
        load.wait()
    picked = dot(lev_ref[...].reshape(8 * ROWS, LEVEL).astype(F32).astype(BF16), pick_ref[...])
    for d in order:
        above = (mod(z + d, 8) > z).astype(jnp.int32)
        keep = jnp.broadcast_to(kind <= above, (ROWS, DEPTH))
        bsend[d - 1] = fold(jnp.where(keep, picked[ROWS * d : ROWS * d + ROWS], -1.0), 256)
    own = 24 * me + lax.broadcasted_iota(jnp.int32, (ROWS, DEPTH), 0)
    codes_ref[pl.ds(0, ROWS), :] = jnp.where((kind < 2) & (source > own), picked[:ROWS], -1.0)
    codes_ref[pl.ds(ROWS, ROWS), :] = jnp.where((kind < 1) & (source < own), picked[:ROWS], -1.0)
    for d in order:
        n = slot_of[8 - d]
        remote(bsend.at[d - 1], brecv.at[n], c_send, c_recv.at[n], device(0, 0, d, 0)).start()

    def set_rows(slot, rows, sign):
        tiles = [rows[:, 128 * t : 128 * t + 128] for t in range(3)]
        at = pl.ds(pl.multiple_of(ROWS * slot, 8), ROWS)
        for t, (one, two) in enumerate(zip(tiles, swap(tiles))):
            wa_ref[at, pl.ds(128 * t, 128)] = one
            wa_ref[at, pl.ds(384 + 128 * t, 128)] = two * sign

    def block_of(ref):
        return unfold(ref[...], 384, 256)

    bins = lax.broadcasted_iota(jnp.int32, (64, 128), 0).astype(F32).astype(BF16)

    def one_hots(out, slot, part):
        codes = codes_ref[pl.ds(pl.multiple_of(ROWS * slot, 8), ROWS), :]
        for a in range(12):
            row = codes[12 * part + a : 12 * part + a + 1]
            for t in range(4):
                lanes = pl.ds(128 * t, 128)
                code = jnp.broadcast_to(row[:, 128 * t : 128 * t + 128], (16, 128)).astype(BF16)
                for k in range(4):
                    out[pl.ds(64 * a + 16 * k, 16), lanes] = jnp.where(
                        code == bins[16 * k : 16 * k + 16], jnp.ones((), BF16), jnp.zeros((), BF16)
                    )

    def take(slot, part, ref):
        rows = pl.ds(pl.multiple_of(ROWS * slot, 8), ROWS)
        for t in range(3):
            lanes, more = pl.ds(128 * t, 128), pl.ds(384 + 128 * t, 128)
            w, v = wa_ref[rows, lanes], wa_ref[rows, more]
            xs, ys = x_acc[:, lanes], y_acc[:, lanes]
            for a in range(12):
                at = 12 * part + a
                piece = ref[pl.ds(64 * a, 64), lanes]
                xs = xs + w[at : at + 1] * piece
                ys = ys + v[at : at + 1] * piece
            x_acc[:, lanes] = xs
            y_acc[:, lanes] = ys

    def start(slot, carry):
        for part in range(2):
            at = pl.multiple_of(ROWS * NBINS * slot + 12 * NBINS * part, 16)
            one_hots(hot_own.at[pl.ds(at, 12 * NBINS)], slot, part)
        return carry

    lax.fori_loop(0, 2, start, 0)
    rows = block_of(mine)
    set_rows(0, rows, 1.0)
    set_rows(1, rows, -1.0)
    x_acc[...] = jnp.zeros_like(x_acc)
    y_acc[...] = jnp.zeros_like(y_acc)
    s1[...] = jnp.zeros_like(s1)
    loads["lag"].wait()
    lag_hi, lag_lo = halves(lag_ref[...])
    lhi_ref[...] = lag_hi
    llo_ref[...] = lag_lo
    for far in range(2):
        bmat[pl.ds(DEPTH // 2 * far + 240, 16), :] = jnp.zeros((16, 384), BF16)

    groups = (pl.ds(FAR, blocks - FAR), pl.ds(0, FAR))
    near = bbuf.at[0, pl.ds(FAR, blocks - 1 - FAR)]
    far = bbuf.at[0, pl.ds(0, FAR)]

    def share(k):
        at = groups[k]
        return remote(bbuf.at[0, at], bbuf.at[1, at], s_send, s_recv.at[k], sibling)

    def assemble(far):
        for i in range(FAR):
            two = [block_of(bbuf.at[m // FAR, m % FAR + FAR * (1 - far)]) for m in (2 * i, 2 * i + 1)]
            bmat[pl.ds(DEPTH // 2 * far + 2 * ROWS * i, 2 * ROWS), :] = jnp.concatenate(two, axis=0).astype(BF16)

    remote(near, near, b_send, b_recv.at[1], sibling).wait_recv()
    share(0).start()
    share(0).wait_recv()
    assemble(0)
    remote(far, far, b_send, b_recv.at[0], sibling).wait_recv()
    share(1).start()

    def own_body(step, carry):
        far, slot = lax.div(step, jnp.int32(2)), mod(step, 2)

        @pl.when(step == 2)
        def _():
            share(1).wait_recv()
            assemble(1)

        @pl.when(step == 3)
        def _():
            wait_codes(0)
            put_codes(0)

        half = pl.ds(pl.multiple_of(DEPTH // 2 * far, 256), DEPTH // 2)
        at = pl.multiple_of(ROWS * NBINS * slot, 16)
        s0[...] = dot(hot_own[pl.ds(at, 12 * NBINS), half], bmat[half, :])
        take(1 - slot, 1, s1)
        s1[...] = dot(hot_own[pl.ds(at + 12 * NBINS, 12 * NBINS), half], bmat[half, :])
        one_hots(hot0, 2, 0)
        take(slot, 0, s0)
        return carry

    def wait_codes(n):
        remote(brecv.at[n], brecv.at[n], c_send, c_recv.at[n], sibling).wait_recv()

    def put_codes(n):
        codes_ref[pl.ds(pl.multiple_of(ROWS * (n + 2), 8), ROWS), :] = unfold(brecv[n], 512, 256)

    lax.fori_loop(0, 4, own_body, 0)

    def body(slot, carry):
        @pl.when(slot < 8)
        def _():
            wait_codes(slot - 1)

        n, m = slot - 2, jnp.minimum(slot - 1, 6)
        remote(abuf.at[n], abuf.at[n], a_send, a_recv.at[n], sibling).wait_recv()
        s0[...] = dot(hot0[...], bmat[...])
        one_hots(hot1, slot, 1)
        take(slot - 1, 1, s1)
        put_codes(m)
        k = lax.div(slot, jnp.int32(2))
        d = k + mod(slot, 2) * (8 - 2 * k)
        below = (mod(z + d, 8) < z).astype(F32)
        set_rows(slot, block_of(abuf.at[n]), 2.0 * below - 1.0)
        s1[...] = dot(hot1[...], bmat[...])
        one_hots(hot0, m + 2, 0)
        take(slot, 0, s0)
        return carry

    lax.fori_loop(2, 9, body, 0)
    take(8, 1, s1)

    xs = [x_acc[:, pl.ds(128 * t, 128)] for t in range(3)]
    ys = [y_acc[:, pl.ds(128 * t, 128)] for t in range(3)]
    sums = [xs[0] + xs[2], xs[1] + unpack(xs, 64), ys[0] - ys[2], ys[1] - unpack(ys, 64)]
    for t in range(4):
        for k in range(8):
            part[k, t] = sums[t][8 * k : 8 * k + 8]

    at = 4 * place + quad
    r1[at] = part[place, quad]
    for n, (dx, dy, dc) in enumerate(plane):
        to = device(dx, dy, 0, dc)
        remote(part.at[to[1], mod(to[0], 4)], r1.at[at], r1_send, r1_recv, to).start()
    remote(r1.at[pl.ds(0, 31)], r1.at[pl.ds(0, 31)], r1_send, r1_recv, sibling).wait_recv()

    def total(ref, n):
        values = [ref[i] for i in range(n)]
        while len(values) > 1:
            values = [a + b for a, b in zip(values[::2], values[1::2])]
        return values[0]

    r2[y_lo, z] = total(r1, 32)
    for d in (4, 3, 5, 2, 6, 1, 7, 0):
        for e in (other, 0) if d else (other,):
            remote(r2.at[y_lo, z], r2.at[y_lo, z], r2_send, r2_recv, device(0, e, d, 0)).start()
    most = r1.at[pl.ds(0, 15)]
    remote(most, most, r2_send, r2_recv, sibling).wait_recv()
    for k in range(2):
        r3[core, k] = total(r2.at[k], 8)
    remote(r3.at[core], r3.at[core], r3_send, r3_recv, sibling).start()
    remote(r3.at[core], r3.at[core], r3_send, r3_recv, sibling).wait_recv()
    hi, lo = halves(jnp.concatenate([r3[t % 2, t // 2] for t in range(4)], axis=1))
    both = jnp.concatenate([hi.astype(F32), lo.astype(F32)], axis=0).astype(BF16)
    out = dot(both, lhi_ref[...]) + dot(both, llo_ref[...])
    out_ref[...] = out[:8] + out[8:]
    for src, send, recv in (
        (bbuf.at[0, pl.ds(0, blocks - 1)], b_send, b_recv.at[0]), (bbuf.at[0], s_send, s_recv.at[0]), (abuf, a_send, a_recv.at[0]), (bsend, c_send, c_recv.at[0]),
        (r1.at[pl.ds(0, 31)], r1_send, r1_recv), (most, r2_send, r2_recv), (r3.at[0], r3_send, r3_recv),
    ):
        remote(src, src, send, recv, sibling).wait_send()


def solution(mesh):
    tables = make_tables()
    any_space = pl.BlockSpec(memory_space=pl.ANY)
    vmem = pl.BlockSpec(memory_space=pltpu.VMEM)
    dma = pltpu.SemaphoreType.DMA

    def step(traces, fir_taps, pair_bin):
        return pl.pallas_call(
            kernel,
            out_shape=jax.ShapeDtypeStruct((8, LAGS), F32),
            in_specs=[any_space, vmem, any_space] + [any_space] * len(tables),
            out_specs=vmem,
            scratch_shapes=[
                pltpu.VMEM((ROWS, SAMPLES), F32),
                *[pltpu.VMEM(t.shape, t.dtype) for t in tables],
                pltpu.VMEM((8, ROWS, LEVEL), jnp.int32),
                pltpu.VMEM((LEVEL, DEPTH), BF16),
                pltpu.VMEM((16 * ROWS, 512), BF16),
                pltpu.VMEM((16 * ROWS, 512), BF16),
                pltpu.VMEM((512, 512), BF16),
                pltpu.VMEM((512, 512), BF16),
                pltpu.VMEM((2, len(HALF), 16, 640), BF16),
                pltpu.VMEM((7, 16, 640), BF16),
                pltpu.VMEM((7, 16, 768), BF16),
                pltpu.VMEM((7, 16, 768), BF16),
                pltpu.VMEM((9 * ROWS, DEPTH), F32),
                pltpu.VMEM((9 * ROWS, 768), F32),
                pltpu.VMEM((2 * ROWS * NBINS, DEPTH), BF16),
                pltpu.VMEM((12 * NBINS, DEPTH), BF16),
                pltpu.VMEM((12 * NBINS, DEPTH), BF16),
                pltpu.VMEM((DEPTH, 384), BF16),
                pltpu.VMEM((12 * NBINS, 384), F32),
                pltpu.VMEM((12 * NBINS, 384), F32),
                pltpu.VMEM((64, 384), F32),
                pltpu.VMEM((64, 384), F32),
                pltpu.VMEM((8, 4, 8, 128), F32),
                pltpu.VMEM((32, 8, 128), F32),
                pltpu.VMEM((2, 8, 8, 128), F32),
                pltpu.VMEM((2, 2, 8, 128), F32),
                dma((7,)),
                dma((8,)),
                dma(()),
                dma((2,)),
                dma(()),
                dma((2,)),
                dma(()),
                dma((7,)),
                dma(()),
                dma((7,)),
                dma(()),
                dma(()),
                dma(()),
                dma(()),
                dma(()),
                dma(()),
            ],
            compiler_params=pltpu.CompilerParams(
                collective_id=0, has_side_effects=True, vmem_limit_bytes=56 * 2**20
            ),
            name="stack",
        )(traces, fir_taps.reshape(1, TAPS), pair_bin, *[jnp.asarray(t) for t in tables])

    return jax.shard_map(
        step,
        mesh=mesh,
        in_specs=(P(("chan", "bin"), None), P(), P(("chan", "bin"), None)),
        out_specs=P("bin", None),
        check_vma=False,
    )
```

```python
import math

import jax
import jax.numpy as jnp
import numpy as np
from jax import lax
from jax.experimental import pallas as pl
from jax.experimental.pallas import tpu as pltpu
from jax.sharding import PartitionSpec as P

SAMPLES = 4096
TAPS = 64
BAND_LO = 64
NF = 192
MARGIN = 32
LAGS = 512
NBINS = 64
ROWS = 24
LEVEL = 768
MESH = pl.DeviceIdType.MESH
F32 = jnp.float32
BF16 = jnp.bfloat16


def lane_freqs():
    lane = np.arange(128)
    return np.concatenate([16 * (lane % 16) + 8 * j + lane // 16 for j in range(2)])


HALF = [(2, 2), (1, 2), (2, 3), (3, 1), (3, 3), (2, 0), (0, 2), (1, 0), (0, 1), (0, 0)]
FAR = 5
DEPTH = 512


def geometry():
    table = np.zeros((8, DEPTH), np.int32)
    table[3], table[4] = -4096, 2
    for far, dc, n in np.ndindex(2, 2, FAR):
        start = DEPTH // 2 * far + ROWS * (FAR * dc + n)
        at = slice(start, start + ROWS)
        h = HALF[n + FAR * (1 - far)]
        table[:3, at] = np.array((*h, dc))[:, None]
        table[3, at] = np.arange(ROWS)
        table[4, at] = not any(v % 2 for v in h)
    return table


def make_tables():
    e = lane_freqs()
    u = np.arange(256)
    ang = 2 * math.pi / SAMPLES * ((u[None, :] * np.arange(16)[:, None]) % SAMPLES)
    twiddle = np.concatenate([np.cos(ang), np.sin(ang)], 0).astype(np.float32)
    p = 2 + np.arange(128) % 16
    ang = 2 * math.pi / 256 * ((u[:, None] * p[None, :]) % 256)
    c, s = np.cos(ang), np.sin(ang)
    fine = np.concatenate([c, s], 1)
    ang = 2 * math.pi / SAMPLES * ((np.arange(TAPS)[:, None] * (32 + e)[None, :]) % SAMPLES)
    taps = np.concatenate([np.cos(ang), -np.sin(ang)], 1)
    f = e - MARGIN
    ok = (f >= 0) & (f < NF)
    phase = ((BAND_LO + np.where(ok, f, 0))[:, None] * (np.arange(LAGS) - LAGS // 2)[None, :]) % SAMPLES
    ang = 2 * math.pi / SAMPLES * phase
    lag = np.concatenate([np.cos(ang), -np.sin(ang)], 0) * (2.0 / SAMPLES) * np.concatenate([ok, ok])[:, None]
    return [t.astype(np.float32) for t in (twiddle, fine, taps, lag)] + [geometry()]


def dot(a, b, **kw):
    return jnp.dot(a, b, preferred_element_type=F32, **kw)


def halves(a):
    hi = a.astype(BF16)
    return hi, (a - hi.astype(F32)).astype(BF16)


def sixteen(x):
    root = math.sqrt(0.5)
    a = [x[k] + x[k + 8] for k in range(8)]
    b = [x[k] - x[k + 8] for k in range(8)]
    c = [a[k] + a[k + 4] for k in range(4)]
    d = [a[k] - a[k + 4] for k in range(4)]
    y = [None] * 9
    zero = jnp.zeros_like(x[0])
    even, odd = c[0] + c[2], c[1] + c[3]
    y[0] = (even + odd, zero)
    y[8] = (even - odd, zero)
    y[4] = (c[0] - c[2], c[3] - c[1])
    m, n = (d[1] - d[3]) * root, (d[1] + d[3]) * root
    y[2] = (d[0] + m, -(n + d[2]))
    y[6] = (d[0] - m, d[2] - n)
    for r in (1, 3, 5, 7):
        re, im = b[0], b[4] * (-1.0 if r % 4 == 1 else 1.0)
        for k in (1, 2, 3):
            re = re + (b[k] - b[8 - k]) * math.cos(math.pi * k * r / 8)
            im = im - (b[k] + b[8 - k]) * math.sin(math.pi * k * r / 8)
        y[r] = (re, im)
    return y


def freq_of(shape, axis):
    i = lax.broadcasted_iota(jnp.int32, shape, axis)
    return 16 * (i & 15) + 8 * (i >> 7) + ((i >> 4) & 7)


def whiten(x_ref, taps, tw_ref, fine_ref, tap_table, hi_ref, lo_ref, loads):
    padded = jnp.concatenate([taps, jnp.zeros((1, 64), F32)], axis=1)
    shifted = pltpu.roll(jnp.broadcast_to(padded, (128, 128)), 0, 1, stride=1, stride_axis=0)
    target = freq_of((256, 256), 1)
    apart = freq_of((256, 256), 0) - target
    win = jnp.where((apart >= -MARGIN) & (apart < MARGIN), 0.5 / MARGIN, 0.0).astype(BF16)
    loads["taps"].wait()
    gains = dot(shifted[:, :TAPS], tap_table[...], precision=lax.Precision.HIGHEST)
    tail_hi, tail_lo = halves(gains[TAPS:])
    right_cut = jnp.concatenate([tail_hi, tail_hi, tail_lo, jnp.zeros_like(tail_hi)], axis=0)
    loads["x"].wait()
    last = x_ref[:, pl.ds(SAMPLES - 128, 128)]
    last_hi = last.astype(BF16).astype(F32)
    first_lanes = lax.broadcasted_iota(jnp.int32, (24, 128), 1) < 64
    moved = pltpu.roll(last_hi, 64, 1)
    pieces = [jnp.where(first_lanes, moved, last - last_hi), jnp.where(first_lanes, moved, 0.0)]
    left_cut = jnp.concatenate(pieces, axis=1).astype(BF16)
    loads["tw"].wait()

    def body(i, carry):
        rows = pl.ds(pl.multiple_of(8 * i, 8), 8)
        for j in range(2):
            lanes = pl.ds(128 * j, 128)
            y = sixteen([x_ref[rows, pl.ds(256 * w + 128 * j, 128)] for w in range(16)])
            parts = []
            for r in range(16):
                re, im = y[min(r, 16 - r)]
                if r > 8:
                    im = -im
                if r:
                    c, s = tw_ref[pl.ds(r, 1), lanes], tw_ref[pl.ds(16 + r, 1), lanes]
                    re, im = re * c + im * s, im * c - re * s
                parts.append((re, im))
            for r in range(0, 16, 2):
                at = pl.ds(pl.multiple_of(128 * i + 8 * r, 16), 16)
                for k in range(2):
                    hi, lo = halves(jnp.concatenate([parts[r][k], parts[r + 1][k]], axis=0))
                    hi_ref[at, pl.ds(256 * k + 128 * j, 128)] = hi
                    lo_ref[at, pl.ds(256 * k + 128 * j, 128)] = lo
        return carry

    lax.fori_loop(0, 3, body, 0)
    loads["fine"].wait()
    both = fine_ref[...]
    c, s = halves(both[:, :128]), halves(both[:, 128:])
    fine = [jnp.concatenate([jnp.concatenate([c[k], -s[k]], 1), jnp.concatenate([s[k], c[k]], 1)], 0) for k in range(2)]
    left = jnp.concatenate([hi_ref[...], lo_ref[...], hi_ref[...]], axis=1)
    z = dot(left, jnp.concatenate([fine[0], fine[0], fine[1]], axis=0))
    lane = lax.broadcasted_iota(jnp.int32, (24, 128), 1)
    ext = []
    for part in range(2):
        for j in range(2):
            tile = jnp.zeros((24, 128), F32)
            for r in range(8):
                at = 8 * (8 * j + r)
                piece = jnp.concatenate([z[128 * i + at : 128 * i + at + 8, 128 * part : 128 * part + 128] for i in range(3)], 0)
                tile = jnp.where(lane // 16 == r, piece, tile)
            ext.append(tile)
    cut = dot(left_cut, right_cut)
    h = [gains[0:1, 128 * k : 128 * k + 128] for k in range(4)]
    re = [h[j] * ext[j] - h[2 + j] * ext[2 + j] - cut[:, 128 * j : 128 * j + 128] for j in range(2)]
    im = [h[j] * ext[2 + j] + h[2 + j] * ext[j] - cut[:, 256 + 128 * j : 384 + 128 * j] for j in range(2)]
    power = jnp.concatenate([re[j] * re[j] + im[j] * im[j] for j in range(2)], axis=1)
    one = power.astype(BF16).astype(F32)
    two = (power - one).astype(BF16).astype(F32)
    sums = dot(jnp.concatenate([one, two, power - one - two], axis=0).astype(BF16), win)
    smooth = sums[:24] + sums[24:48] + sums[48:]
    scale = 1.0 / jnp.sqrt(smooth + 1e-06)
    r0, r1 = (re[j] * scale[:, 128 * j : 128 * j + 128] for j in range(2))
    i0, i1 = (im[j] * scale[:, 128 * j : 128 * j + 128] for j in range(2))
    slot = lane % 16
    band = (slot >= 2) & (slot < 14)

    def pack(a, b, c, d):
        return [
            jnp.where(band, t, pltpu.roll(d, s, 1)) for t, s in ((a, 12), (b, 8), (c, 4))
        ]

    return pack(r0, r1, i0, i1)


def swap(tiles):
    a, b, c = tiles
    slot = lax.broadcasted_iota(jnp.int32, (ROWS, 128), 1) % 16
    band = (slot >= 2) & (slot < 14)
    full = (c, unpack(tiles, ROWS), a)
    return [jnp.where(band, t, pltpu.roll(b, s, 1)) for t, s in zip(full, (12, 8, 4))]


def unpack(tiles, rows):
    slot = lax.broadcasted_iota(jnp.int32, (rows, 128), 1) % 16
    a, b, c = (pltpu.roll(t, s, 1) for t, s in zip(tiles, (116, 120, 124)))
    return jnp.where(slot < 6, a, jnp.where(slot < 10, b, c))


def mod(a, n):
    return lax.rem(a, jnp.int32(n))


def fold(rows, width):
    parts = [rows[16:, i : i + width] for i in range(0, rows.shape[1], width)]
    if parts[1].shape[1] < width:
        parts[1] = jnp.concatenate([parts[1], jnp.zeros((8, width - parts[1].shape[1]), F32)], axis=1)
    return jnp.concatenate([rows[:16], jnp.concatenate(parts, axis=0)], axis=1).astype(BF16)


def unfold(block, cols, width):
    wide = block.astype(F32)
    tail = [wide[:8, cols:], wide[8:, cols : 2 * cols - width]]
    return jnp.concatenate([wide[:, :cols], jnp.concatenate(tail, axis=1)], axis=0)


def kernel(
    x_hbm, taps_ref, bins_hbm, tw_hbm, fine_hbm, tap_hbm, lag_hbm, geo_hbm,
    out_ref,
    x_ref, tw_ref, fine_ref, tap_ref, lag_ref, geo_ref, lev_ref, pick_ref, hi_ref, lo_ref, lhi_ref, llo_ref,
    bbuf, abuf, bsend, brecv, codes_ref, wa_ref, hot_own, hot0, hot1, bmat, s0, s1, x_acc, y_acc, part, r1, r2, r3,
    in_sem, lev_sem, b_send, b_recv, s_send, s_recv, a_send, a_recv, c_send, c_recv,
    r1_send, r1_recv, r2_send, r2_recv, r3_send, r3_recv,
):
    chan, place = lax.axis_index("chan"), lax.axis_index("bin")
    z, quad = lax.div(chan, jnp.int32(4)), mod(chan, 4)
    y_lo, core = lax.div(quad, jnp.int32(2)), mod(quad, 2)
    y_hi, x = lax.div(place, jnp.int32(4)), mod(place, 4)
    y = 2 * y_hi + y_lo
    me = 16 * y_lo + 8 * core + place

    def device(dx, dy, dz, dc):
        xx, yy, zz, cc = mod(x + dx, 4), mod(y + dy, 4), mod(z + dz, 8), mod(core + dc, 2)
        return (4 * zz + 2 * mod(yy, 2) + cc, 4 * lax.div(yy, jnp.int32(2)) + xx)

    lev_loads = [
        pltpu.make_async_copy(
            bins_hbm.at[:, pl.ds(pl.multiple_of(mod(z + d, 8) * LEVEL, 128), LEVEL)], lev_ref.at[d], lev_sem.at[d]
        )
        for d in range(8)
    ]
    copies = dict(
        taps=(tap_hbm, tap_ref), x=(x_hbm, x_ref), tw=(tw_hbm, tw_ref), fine=(fine_hbm, fine_ref),
        geo=(geo_hbm, geo_ref), lag=(lag_hbm, lag_ref),
    )
    loads = {name: pltpu.make_async_copy(*refs, in_sem.at[i]) for i, (name, refs) in enumerate(copies.items())}
    for name in ("x", "tw", "taps", "fine", "geo"):
        loads[name].start()
    for load in lev_loads:
        load.start()

    other = 1 - 2 * y_lo
    plane = [h for h in np.ndindex(4, 4, 2) if any(h)]
    plane.sort(key=lambda h: -(min(h[0], 4 - h[0]) + min(h[1], 4 - h[1])))
    plane = [tuple(map(int, h)) for h in plane]
    friends = [device(0, e, d, 0) for d in (4, 3, 5) for e in (other, 0)]
    friends += [device(dx, dy, 0, dc) for dx, dy, dc in plane]
    friends += [device(0, e, d, 0) for d in (2, 6, 1, 7) for e in (other, 0)]
    barrier = pltpu.get_barrier_semaphore()
    for friend in friends:
        pl.semaphore_signal(barrier, inc=1, device_id=friend, device_id_type=MESH)

    def remote(src, dst, send, recv, to):
        return pltpu.make_async_remote_copy(
            src_ref=src, dst_ref=dst, send_sem=send, recv_sem=recv, device_id=to, device_id_type=MESH
        )

    sibling = device(0, 0, 0, 1)
    white = whiten(x_ref, taps_ref[...], tw_ref, fine_ref, tap_ref, hi_ref, lo_ref, loads)
    blocks = len(HALF)
    mine = bbuf.at[0, blocks - 1]
    mine[...] = fold(jnp.concatenate(white, axis=1), 256)

    pl.semaphore_wait(barrier, len(friends))
    order = (1, 7, 2, 6, 3, 5, 4)
    slot_of = {d: n for n, d in enumerate(order)}
    for n, (dx, dy) in enumerate(HALF[:-1]):
        remote(mine, bbuf.at[0, n], b_send, b_recv.at[int(n >= FAR)], device(4 - dx, 4 - dy, 0, 0)).start()

    for d in order:
        n = slot_of[8 - d]
        remote(mine, abuf.at[n], a_send, a_recv.at[n], device(0, 0, d, 0)).start()

    loads["lag"].start()
    loads["geo"].wait()
    dx, dy, dc = (geo_ref[pl.ds(i, 1), :] for i in range(3))
    kind = geo_ref[pl.ds(4, 1), :]
    xx, yy, cc = (x + dx) & 3, (y + dy) & 3, (core + dc) & 1
    source = 24 * (16 * (yy & 1) + 8 * cc + 4 * (yy >> 1) + xx) + geo_ref[pl.ds(3, 1), :]
    pick_ref[...] = (lax.broadcasted_iota(jnp.int32, (LEVEL, DEPTH), 0) == source).astype(F32).astype(BF16)
    for load in lev_loads:
        load.wait()
    picked = dot(lev_ref[...].reshape(8 * ROWS, LEVEL).astype(F32).astype(BF16), pick_ref[...])
    for d in order:
        above = (mod(z + d, 8) > z).astype(jnp.int32)
        keep = jnp.broadcast_to(kind <= above, (ROWS, DEPTH))
        bsend[d - 1] = fold(jnp.where(keep, picked[ROWS * d : ROWS * d + ROWS], -1.0), 256)
    own = 24 * me + lax.broadcasted_iota(jnp.int32, (ROWS, DEPTH), 0)
    codes_ref[pl.ds(0, ROWS), :] = jnp.where((kind < 2) & (source > own), picked[:ROWS], -1.0)
    codes_ref[pl.ds(ROWS, ROWS), :] = jnp.where((kind < 1) & (source < own), picked[:ROWS], -1.0)
    for d in order:
        n = slot_of[8 - d]
        remote(bsend.at[d - 1], brecv.at[n], c_send, c_recv.at[n], device(0, 0, d, 0)).start()

    def set_rows(slot, rows, sign):
        tiles = [rows[:, 128 * t : 128 * t + 128] for t in range(3)]
        at = pl.ds(pl.multiple_of(ROWS * slot, 8), ROWS)
        for t, (one, two) in enumerate(zip(tiles, swap(tiles))):
            wa_ref[at, pl.ds(128 * t, 128)] = one
            wa_ref[at, pl.ds(384 + 128 * t, 128)] = two * sign

    def block_of(ref):
        return unfold(ref[...], 384, 256)

    bins = lax.broadcasted_iota(jnp.int32, (64, 128), 0).astype(F32).astype(BF16)

    def one_hots(out, slot, part):
        codes = codes_ref[pl.ds(pl.multiple_of(ROWS * slot, 8), ROWS), :]
        for a in range(12):
            row = codes[12 * part + a : 12 * part + a + 1]
            for t in range(4):
                lanes = pl.ds(128 * t, 128)
                code = jnp.broadcast_to(row[:, 128 * t : 128 * t + 128], (16, 128)).astype(BF16)
                for k in range(4):
                    out[pl.ds(64 * a + 16 * k, 16), lanes] = jnp.where(
                        code == bins[16 * k : 16 * k + 16], jnp.ones((), BF16), jnp.zeros((), BF16)
                    )

    def take(slot, part, ref):
        rows = pl.ds(pl.multiple_of(ROWS * slot, 8), ROWS)
        for t in range(3):
            lanes, more = pl.ds(128 * t, 128), pl.ds(384 + 128 * t, 128)
            w, v = wa_ref[rows, lanes], wa_ref[rows, more]
            xs, ys = x_acc[:, lanes], y_acc[:, lanes]
            for a in range(12):
                at = 12 * part + a
                piece = ref[pl.ds(64 * a, 64), lanes]
                xs = xs + w[at : at + 1] * piece
                ys = ys + v[at : at + 1] * piece
            x_acc[:, lanes] = xs
            y_acc[:, lanes] = ys

    def start(slot, carry):
        for part in range(2):
            at = pl.multiple_of(ROWS * NBINS * slot + 12 * NBINS * part, 16)
            one_hots(hot_own.at[pl.ds(at, 12 * NBINS)], slot, part)
        return carry

    lax.fori_loop(0, 2, start, 0)
    rows = block_of(mine)
    set_rows(0, rows, 1.0)
    set_rows(1, rows, -1.0)
    x_acc[...] = jnp.zeros_like(x_acc)
    y_acc[...] = jnp.zeros_like(y_acc)
    s1[...] = jnp.zeros_like(s1)
    loads["lag"].wait()
    lag_hi, lag_lo = halves(lag_ref[...])
    lhi_ref[...] = lag_hi
    llo_ref[...] = lag_lo
    for far in range(2):
        bmat[pl.ds(DEPTH // 2 * far + 240, 16), :] = jnp.zeros((16, 384), BF16)

    groups = (pl.ds(FAR, blocks - FAR), pl.ds(0, FAR))
    near = bbuf.at[0, pl.ds(FAR, blocks - 1 - FAR)]
    far = bbuf.at[0, pl.ds(0, FAR)]

    def share(k):
        at = groups[k]
        return remote(bbuf.at[0, at], bbuf.at[1, at], s_send, s_recv.at[k], sibling)

    def assemble(far):
        for i in range(FAR):
            two = [block_of(bbuf.at[m // FAR, m % FAR + FAR * (1 - far)]) for m in (2 * i, 2 * i + 1)]
            bmat[pl.ds(DEPTH // 2 * far + 2 * ROWS * i, 2 * ROWS), :] = jnp.concatenate(two, axis=0).astype(BF16)

    remote(near, near, b_send, b_recv.at[1], sibling).wait_recv()
    share(0).start()
    remote(far, far, b_send, b_recv.at[0], sibling).wait_recv()
    share(1).start()
    share(0).wait_recv()
    assemble(0)

    def own_body(step, carry):
        far, slot = lax.div(step, jnp.int32(2)), mod(step, 2)

        @pl.when(step == 2)
        def _():
            share(1).wait_recv()
            assemble(1)

        @pl.when(step == 3)
        def _():
            wait_codes(0)
            put_codes(0)

        half = pl.ds(pl.multiple_of(DEPTH // 2 * far, 256), DEPTH // 2)
        at = pl.multiple_of(ROWS * NBINS * slot, 16)
        s0[...] = dot(hot_own[pl.ds(at, 12 * NBINS), half], bmat[half, :])
        take(1 - slot, 1, s1)
        s1[...] = dot(hot_own[pl.ds(at + 12 * NBINS, 12 * NBINS), half], bmat[half, :])
        one_hots(hot0, 2, 0)
        take(slot, 0, s0)
        return carry

    def wait_codes(n):
        remote(brecv.at[n], brecv.at[n], c_send, c_recv.at[n], sibling).wait_recv()

    def put_codes(n):
        codes_ref[pl.ds(pl.multiple_of(ROWS * (n + 2), 8), ROWS), :] = unfold(brecv[n], 512, 256)

    lax.fori_loop(0, 4, own_body, 0)

    def body(slot, carry):
        @pl.when(slot < 8)
        def _():
            wait_codes(slot - 1)

        n, m = slot - 2, jnp.minimum(slot - 1, 6)
        remote(abuf.at[n], abuf.at[n], a_send, a_recv.at[n], sibling).wait_recv()
        s0[...] = dot(hot0[...], bmat[...])
        one_hots(hot1, slot, 1)
        take(slot - 1, 1, s1)
        put_codes(m)
        k = lax.div(slot, jnp.int32(2))
        d = k + mod(slot, 2) * (8 - 2 * k)
        below = (mod(z + d, 8) < z).astype(F32)
        set_rows(slot, block_of(abuf.at[n]), 2.0 * below - 1.0)
        s1[...] = dot(hot1[...], bmat[...])
        one_hots(hot0, m + 2, 0)
        take(slot, 0, s0)
        return carry

    lax.fori_loop(2, 9, body, 0)
    take(8, 1, s1)

    xs = [x_acc[:, pl.ds(128 * t, 128)] for t in range(3)]
    ys = [y_acc[:, pl.ds(128 * t, 128)] for t in range(3)]
    sums = [xs[0] + xs[2], xs[1] + unpack(xs, 64), ys[0] - ys[2], ys[1] - unpack(ys, 64)]
    for t in range(4):
        for k in range(8):
            part[k, t] = sums[t][8 * k : 8 * k + 8]

    at = 4 * place + quad
    r1[at] = part[place, quad]
    for n, (dx, dy, dc) in enumerate(plane):
        to = device(dx, dy, 0, dc)
        remote(part.at[to[1], mod(to[0], 4)], r1.at[at], r1_send, r1_recv, to).start()
    remote(r1.at[pl.ds(0, 31)], r1.at[pl.ds(0, 31)], r1_send, r1_recv, sibling).wait_recv()

    def total(ref, n):
        values = [ref[i] for i in range(n)]
        while len(values) > 1:
            values = [a + b for a, b in zip(values[::2], values[1::2])]
        return values[0]

    r2[y_lo, z] = total(r1, 32)
    for d in (4, 3, 5, 2, 6, 1, 7, 0):
        for e in (other, 0) if d else (other,):
            remote(r2.at[y_lo, z], r2.at[y_lo, z], r2_send, r2_recv, device(0, e, d, 0)).start()
    most = r1.at[pl.ds(0, 15)]
    remote(most, most, r2_send, r2_recv, sibling).wait_recv()
    for k in range(2):
        r3[core, k] = total(r2.at[k], 8)
    remote(r3.at[core], r3.at[core], r3_send, r3_recv, sibling).start()
    remote(r3.at[core], r3.at[core], r3_send, r3_recv, sibling).wait_recv()
    hi, lo = halves(jnp.concatenate([r3[t % 2, t // 2] for t in range(4)], axis=1))
    both = jnp.concatenate([hi.astype(F32), lo.astype(F32)], axis=0).astype(BF16)
    out = dot(both, lhi_ref[...]) + dot(both, llo_ref[...])
    out_ref[...] = out[:8] + out[8:]
    for src, send, recv in (
        (bbuf.at[0, pl.ds(0, blocks - 1)], b_send, b_recv.at[0]), (bbuf.at[0], s_send, s_recv.at[0]), (abuf, a_send, a_recv.at[0]), (bsend, c_send, c_recv.at[0]),
        (r1.at[pl.ds(0, 31)], r1_send, r1_recv), (most, r2_send, r2_recv), (r3.at[0], r3_send, r3_recv),
    ):
        remote(src, src, send, recv, sibling).wait_send()


def solution(mesh):
    tables = make_tables()
    any_space = pl.BlockSpec(memory_space=pl.ANY)
    vmem = pl.BlockSpec(memory_space=pltpu.VMEM)
    dma = pltpu.SemaphoreType.DMA

    def step(traces, fir_taps, pair_bin):
        return pl.pallas_call(
            kernel,
            out_shape=jax.ShapeDtypeStruct((8, LAGS), F32),
            in_specs=[any_space, vmem, any_space] + [any_space] * len(tables),
            out_specs=vmem,
            scratch_shapes=[
                pltpu.VMEM((ROWS, SAMPLES), F32),
                *[pltpu.VMEM(t.shape, t.dtype) for t in tables],
                pltpu.VMEM((8, ROWS, LEVEL), jnp.int32),
                pltpu.VMEM((LEVEL, DEPTH), BF16),
                pltpu.VMEM((16 * ROWS, 512), BF16),
                pltpu.VMEM((16 * ROWS, 512), BF16),
                pltpu.VMEM((512, 512), BF16),
                pltpu.VMEM((512, 512), BF16),
                pltpu.VMEM((2, len(HALF), 16, 640), BF16),
                pltpu.VMEM((7, 16, 640), BF16),
                pltpu.VMEM((7, 16, 768), BF16),
                pltpu.VMEM((7, 16, 768), BF16),
                pltpu.VMEM((9 * ROWS, DEPTH), F32),
                pltpu.VMEM((9 * ROWS, 768), F32),
                pltpu.VMEM((2 * ROWS * NBINS, DEPTH), BF16),
                pltpu.VMEM((12 * NBINS, DEPTH), BF16),
                pltpu.VMEM((12 * NBINS, DEPTH), BF16),
                pltpu.VMEM((DEPTH, 384), BF16),
                pltpu.VMEM((12 * NBINS, 384), F32),
                pltpu.VMEM((12 * NBINS, 384), F32),
                pltpu.VMEM((64, 384), F32),
                pltpu.VMEM((64, 384), F32),
                pltpu.VMEM((8, 4, 8, 128), F32),
                pltpu.VMEM((32, 8, 128), F32),
                pltpu.VMEM((2, 8, 8, 128), F32),
                pltpu.VMEM((2, 2, 8, 128), F32),
                dma((7,)),
                dma((8,)),
                dma(()),
                dma((2,)),
                dma(()),
                dma((2,)),
                dma(()),
                dma((7,)),
                dma(()),
                dma((7,)),
                dma(()),
                dma(()),
                dma(()),
                dma(()),
                dma(()),
                dma(()),
            ],
            compiler_params=pltpu.CompilerParams(
                collective_id=0, has_side_effects=True, vmem_limit_bytes=56 * 2**20
            ),
            name="stack",
        )(traces, fir_taps.reshape(1, TAPS), pair_bin, *[jnp.asarray(t) for t in tables])

    return jax.shard_map(
        step,
        mesh=mesh,
        in_specs=(P(("chan", "bin"), None), P(), P(("chan", "bin"), None)),
        out_specs=P("bin", None),
        check_vma=False,
    )
```
